256 devices in a mesh: grp: 8 (over z), enc: 32 (over y, x, core).
Axes of the slice: x: 4, y: 4, z: 8, core: 2. Of those that a mesh axis runs over, the one named last changes fastest.
Arguments:
- history: bfloat16 [3072, 128, 1024], P(('grp', 'enc')), may hold values from -6 to 6
- hist_len: int32 [3072], P(('grp', 'enc')), may hold values from 0 to 2, as said below
- cand: bfloat16 [131072, 1024], P(('grp', 'enc')), may hold values from -6 to 6
- cand_owner: int32 [131072, 1], P(('grp', 'enc')), may hold values from 0 to 255; in each aligned block of 512 rows (0 to 511, 512 to 1023, ...) at most 3 rows name the same one
- cand_user: int32 [131072], P(('grp', 'enc')), may hold values from 0 to 11
- norm_gain: float32 [1024], replicated, may hold values from 0.1 to 1.9
- w_proj: bfloat16 [1024, 2048], replicated, may hold values from -0.1875 to 0.1875
Outputs:
- kv_cache: bfloat16 [3072, 128, 1024], P(('grp', 'enc'))
- cand_out: bfloat16 [131072, 512], P(('grp', 'enc'))
The draws below stay inside these ranges and needn't reach their ends.
Inputs may be any that keep to these rules, and one draw needn't show every extreme that they name: `hist_len`: blocks of history of each missed user; the first user slot of every device has 2. `cand_owner`: among the 512 candidates of one device no owner device is named more than 3 times.
All inputs are finite; a program needn't handle non-finite values.
Results may differ from the reference program's by a relative error of at most 0.013.
Values may be sent and summed in bfloat16 or wider, within the bound.
A program may use at most 64 MiB of HBM per device.

```python
import math
import jax
import jax.numpy as jnp
import numpy as np
from jax import lax

D = 1024
HEADS = 4
HDIM = 128
PIECE = 64
MAXP = 2
USERS = 12
CAND = 512
HD = 512
CAPC = 3
N_GRP = 8
N_ENC = 32


def draw_hist_len(key, part):
    values = jax.random.randint(key, (N_GRP * N_ENC, USERS), 0, MAXP + 1)
    values = values.at[:, 0].set(MAXP)
    return values.reshape(-1).astype(jnp.int32)


def with_ends(array, stream_key, low, high):
    longest = array.shape.index(max(array.shape))
    spots = []
    for shift in (0, 1):
        where = [jax.random.randint(jax.random.fold_in(stream_key, axis), (), 0, length) for axis, length in enumerate(array.shape)]
        where[longest] = (where[longest] + shift) % array.shape[longest]
        spots.append(tuple(where))
    return array.at[spots[0]].set(low).at[spots[1]].set(high)


def level_of(key, shape, cuts, least, largest):
    level = 1.0
    for dim, parts in cuts:
        heights = jax.random.uniform(jax.random.fold_in(jax.random.fold_in(key, 6), dim), (parts,), jnp.float32, least / len(cuts), largest / len(cuts))
        level = level * jnp.repeat(jnp.exp(heights), shape[dim] // parts).reshape((-1,) + (1,) * (len(shape) - 1 - dim))
    return level


def shared_out(own_key, own, number, rows, amount, top, limit, lean):
    ranking = jax.random.permutation(own_key, amount)
    packed, common = shares(amount, rows * top, limit, lean, True), shares(amount, rows * top, limit, lean, False)
    places = jnp.arange(amount)

    def named(sizes, turn):
        used = int((sizes > 0).sum())
        fixed = max(1, used // 4)
        shifted = fixed + (places - fixed + turn * (used - fixed)) % max(1, amount - fixed)
        return jnp.zeros((amount,), jnp.int32).at[ranking[jnp.where(places < fixed, places, shifted)]].set(jnp.asarray(sizes, jnp.int32))

    sizes = jnp.where(number % 4 == 0, named(packed, number // 4), named(common, number - number // 4 - 1))
    mixed = jax.random.permutation(jax.random.fold_in(own, 3), amount)
    giver, taker = mixed[0:amount // 2 * 2:2], mixed[1:amount // 2 * 2:2]
    room = jnp.minimum(sizes[giver] - 1, limit - sizes[taker]) // 2
    room = jnp.where((giver == ranking[0]) | (taker == ranking[0]) | (sizes[taker] == 0), 0, jnp.maximum(room, 0))
    shifted = jax.random.randint(jax.random.fold_in(own, 4), (amount // 2,), 0, 1 << 20) % (room + 1)
    sizes = sizes.at[giver].add(-shifted).at[taker].add(shifted)
    members = jnp.searchsorted(jnp.cumsum(sizes), jnp.arange(rows * top), side="right").astype(jnp.int32)
    grid = members.reshape(top, rows).T
    grid = grid[jax.random.permutation(jax.random.fold_in(own, 1), rows)]
    turn = jax.random.randint(jax.random.fold_in(own, 2), (rows, 1), 0, top)
    return jnp.take_along_axis(grid, (jnp.arange(top)[None, :] + turn) % top, axis=1)


def shares(amount, total, reach, skew, full):
    weights = [(1 << 20) // math.isqrt(rank ** skew) + 1 for rank in range(1, amount + 1)]
    largest = reach if full else min(reach, max(-(-total // amount), total * weights[0] // sum(weights)))
    least = 1 if total - largest >= amount - 1 else 0
    counts, surplus = [largest] + [least] * (amount - 1), total - largest - least * (amount - 1)
    while surplus > 0:
        free = [i for i in range(1, amount) if counts[i] < largest] or [i for i in range(1, amount) if counts[i] < reach]
        mass, budget = sum([weights[i] for i in free]), surplus
        for i in free:
            more = min(reach - counts[i], max(1, budget * weights[i] // mass), surplus)
            counts[i] = counts[i] + more
            surplus = surplus - more
    return np.array(counts)


def normal_values(own_key, extent, scale, reach, pieces=(), held_as=jnp.bfloat16):
    values = jax.random.normal(own_key, extent, jnp.float32) * scale
    if len(pieces) > 0:
        values = level_of(own_key, extent, pieces, -0.22, 0.18) * values
    return jnp.clip(values, min=-reach, max=reach).astype(held_as)


def setup_inputs(seed: int = 0) -> dict:
    key_of = jax.random.split(jax.random.key(seed), 8)
    history = normal_values(key_of[0], (N_GRP * N_ENC * USERS, MAXP * PIECE, D), 1.0, 6.0, ((0, 256),))
    hist_len = draw_hist_len(jax.random.fold_in(key_of[7], 71), 0)
    cand = normal_values(key_of[2], (N_GRP * N_ENC * CAND, D), 1.0, 6.0, ((0, 256),))
    cand_owner_keys = jax.random.split(jax.random.fold_in(key_of[3], 1), (N_GRP * N_ENC * CAND) // CAND)
    cand_owner_turns = jax.random.permutation(jax.random.fold_in(key_of[3], 3), (N_GRP * N_ENC * CAND) // CAND)
    cand_owner = jax.vmap(lambda own, number: shared_out(jax.random.fold_in(key_of[3], 2), own, number, CAND, N_GRP * N_ENC, 1, CAPC, 2))(cand_owner_keys, cand_owner_turns).reshape((N_GRP * N_ENC * CAND, 1))
    cand_user = with_ends(jax.random.randint(key_of[4], (N_GRP * N_ENC * CAND,), 0, USERS), jax.random.fold_in(key_of[4], 1), 0, USERS - 1).astype(jnp.int32)
    norm_gain = jnp.clip(1.0 + 0.18 * jax.random.normal(key_of[5], (D,), jnp.float32), 0.1, 1.9)
    w_proj = normal_values(key_of[6], (D, 4 * HD), D ** -0.5, 0.1875)
    return dict(history=history, hist_len=hist_len, cand=cand, cand_owner=cand_owner, cand_user=cand_user, norm_gain=norm_gain, w_proj=w_proj)


def norm_rows(values):
    center = values - lax.optimization_barrier(jnp.mean(values, axis=-1, keepdims=True))
    spread = lax.optimization_barrier(jnp.mean(center * center, axis=-1, keepdims=True))
    return center * lax.rsqrt(spread + 1e-05)

def encode_users(block, lengths, norm_gain, w_kv):
    normed = (norm_rows(block.astype(jnp.float32)) * norm_gain).astype(jnp.bfloat16)
    mixed = jnp.einsum('urd,de->ure', normed.astype(jnp.float32), w_kv.astype(jnp.float32))
    keyval = jax.nn.silu(mixed).astype(jnp.bfloat16)
    row_ids = jnp.arange(block.shape[1], dtype=jnp.int32)
    live = row_ids[None, :] < (lengths * PIECE)[:, None]
    return jnp.where(live[:, :, None], keyval, jnp.zeros_like(keyval))

def reference(history, hist_len, cand, cand_owner, cand_user, norm_gain, w_proj):
    width = HEADS * HDIM
    w_kv = jnp.concatenate([w_proj[:, 3 * width:], w_proj[:, width:2 * width]], axis=1)
    devices = N_GRP * N_ENC
    rows = MAXP * PIECE
    hist_blocks = history.reshape(devices, USERS, rows, D)
    len_blocks = hist_len.reshape(devices, USERS)
    kv_cache = lax.map(lambda pair: encode_users(pair[0], pair[1], norm_gain, w_kv), (hist_blocks, len_blocks))
    kv_cache = kv_cache.reshape(devices * USERS, rows, 2 * width)
    total = cand.shape[0]
    owner = cand_owner[:, 0]
    user_index = (owner * USERS + cand_user).astype(jnp.int32)
    score_scale = HDIM ** (-0.5)

    def one_block(pack):
        cand_rows, users = pack
        count = cand_rows.shape[0]
        normed = (norm_rows(cand_rows.astype(jnp.float32)) * norm_gain).astype(jnp.bfloat16)
        projected = jax.nn.silu(jnp.dot(normed, w_proj, preferred_element_type=jnp.float32)).astype(jnp.bfloat16)
        gate = projected[:, :width]
        own_v = projected[:, width:2 * width].reshape(count, HEADS, HDIM).astype(jnp.float32)
        query = projected[:, 2 * width:3 * width].reshape(count, HEADS, HDIM).astype(jnp.float32)
        own_k = projected[:, 3 * width:].reshape(count, HEADS, HDIM).astype(jnp.float32)
        stored = kv_cache[users]
        hist_k = stored[:, :, :width].reshape(count, rows, HEADS, HDIM).astype(jnp.float32)
        hist_v = stored[:, :, width:].reshape(count, rows, HEADS, HDIM).astype(jnp.float32)
        scores = jnp.einsum('nhd,nrhd->nhr', query, hist_k) * score_scale
        attention_weight = jax.nn.silu(scores).astype(jnp.bfloat16)
        self_weight = jax.nn.silu(lax.optimization_barrier(jnp.sum(query * own_k, axis=-1)) * score_scale).astype(jnp.bfloat16)
        attended = jnp.einsum('nhr,nrhd->nhd', attention_weight.astype(jnp.float32), hist_v)
        attended = attended + self_weight.astype(jnp.float32)[:, :, None] * own_v
        normed_attn = norm_rows(attended.reshape(count, width)).astype(jnp.bfloat16)
        return (normed_attn.astype(jnp.float32) * gate.astype(jnp.float32)).astype(jnp.bfloat16)
    step = min(CAND, 128)
    cand_out = lax.map(one_block, (cand.reshape(total // step, step, D), user_index.reshape(total // step, step)))
    return (kv_cache, cand_out.reshape(total, width))
```

```python
import functools

import jax
import jax.numpy as jnp
from jax import lax
from jax.experimental import pallas as pl
from jax.experimental.pallas import tpu as pltpu
from jax.sharding import PartitionSpec as P

MESH = pl.DeviceIdType.MESH
HDIM = 128
HEADS = 4
HD = 512
D = 1024
PIECE = 64
ROWS = 128
USERS = 12
CAND = 512
CAP = 3
CHIPS = 128
GROUPS = 4
GSIZE = 32
QROWS = 32
RROWS = 24
BF = jnp.bfloat16
F32 = jnp.float32


def silu(x):
    half = 0.5 * x
    return half + half * jnp.tanh(half)


def norm_rows(x):
    center = x - jnp.mean(x, axis=-1, keepdims=True)
    spread = jnp.mean(center * center, axis=-1, keepdims=True)
    return center * lax.rsqrt(spread + 1e-5)


def dot(a, b):
    return jnp.dot(a, b, preferred_element_type=F32)


def dot_t(a, b):
    return lax.dot_general(a, b, (((1,), (1,)), ((), ())), preferred_element_type=F32)


def kernel(
    len_ref, owner_ref, user_ref, gain_ref, cand_hbm, hist_hbm, w_hbm,
    kv_hbm, out_ref,
    cand_v, hist_v, w_v, kv_v, xn_v, q_v, u_v, self_v, pick_v, place_v,
    tab_own, tab_sib, msg, sib_out, sib_in, land, land_f, ret_f, ret_msg, ret_land, ret_sib,
    back_own, back_sib, back_v,
    load_sem, kv_sem, sib_send, sib_recv, ready_sem,
    q_send, q_recv, r_send, r_recv, f_send, f_recv,
):
    g, e = lax.axis_index("grp"), lax.axis_index("enc")
    y, x, c = e // 8, (e // 2) % 4, e % 2
    sibling = (g, y * 8 + x * 2 + 1 - c)

    def plane_peer(k):
        return g, ((y + k // 4) % 4) * 8 + ((x + k % 4) % 4) * 2 + c

    def peer(idx, sign):
        grp, half, k = idx // 32, (idx // 16) % 2, idx % 16
        dz = (1 - half) * ((4 - grp) % 4) + half * (4 + grp)
        py = (y + sign * (k // 4) + 4) % 4
        px = (x + sign * (k % 4) + 4) % 4
        return (g + sign * dz + 8) % 8, py * 8 + px * 2 + c

    cols = [(2 * HD, 3 * HD), (3 * HD, 4 * HD), (HD, 2 * HD), (0, HD)]
    loads = [pltpu.make_async_copy(cand_hbm, cand_v, load_sem.at[0])]
    for i, (lo, hi) in enumerate(cols):
        loads.append(
            pltpu.make_async_copy(
                w_hbm.at[:, pl.ds(lo, HD)], w_v.at[:, pl.ds(lo, HD)], load_sem.at[1 + i]
            )
        )
    loads.append(pltpu.make_async_copy(hist_hbm, hist_v, load_sem.at[5]))
    for i in (0, 1, 5, 2, 3, 4):
        loads[i].start()

    barrier = pltpu.get_barrier_semaphore()

    def greet_ring(k, carry):
        pl.semaphore_signal(
            barrier, inc=1, device_id=((g + k) % 8, e), device_id_type=MESH
        )
        return carry

    def greet_plane(k, carry):
        pl.semaphore_signal(barrier, inc=1, device_id=plane_peer(k), device_id_type=MESH)
        return carry

    lax.fori_loop(1, 8, greet_ring, 0)
    lax.fori_loop(1, 16, greet_plane, 0)
    pl.semaphore_signal(barrier, inc=1, device_id=sibling, device_id_type=MESH)

    rows_i = lax.broadcasted_iota(jnp.int32, (CAND, CAND), 0)
    cols_i = lax.broadcasted_iota(jnp.int32, (CAND, CAND), 1)
    owner_col = owner_ref[...]
    owner_f = owner_col.astype(F32)
    owner_row = jnp.sum(jnp.where(rows_i == cols_i, owner_f, 0.0), axis=0, keepdims=True)
    same = (owner_f == owner_row) & (cols_i < rows_i)
    rank = jnp.sum(jnp.where(same, 1.0, 0.0), axis=1, keepdims=True).astype(jnp.int32)
    to_g, to_e = owner_col // 32, owner_col % 32
    dz = (to_g - g + 8) % 8
    half = dz // 4
    grp = jnp.where(half == 1, dz - 4, (4 - dz) % 4)
    ry = (to_e // 8 - y + 4) % 4
    rx = ((to_e // 2) % 4 - x + 4) % 4
    other = jnp.where(to_e % 2 == c, 0, 1)
    code_col = (other * CAP + rank) * CHIPS + grp * 32 + half * 16 + ry * 4 + rx
    code_f = code_col.astype(F32)
    code_row = jnp.sum(jnp.where(rows_i == cols_i, code_f, 0.0), axis=0, keepdims=True)
    user_f = user_ref[...].astype(F32)
    user_col = jnp.sum(jnp.where(rows_i == cols_i, user_f, 0.0), axis=1, keepdims=True)
    user_mat = jnp.broadcast_to(user_col, (CAND, HDIM)).astype(BF)
    lane_slot = lax.broadcasted_iota(jnp.int32, (CAND, 2 * CAP * CHIPS), 1).astype(F32)
    place_v[...] = jnp.where(lane_slot == code_f, 1.0, 0.0).astype(BF)
    sub_slot = lax.broadcasted_iota(jnp.int32, (2 * CAP * CHIPS, CAND), 0).astype(F32)
    pick_v[...] = jnp.where(sub_slot == code_row, 1.0, 0.0).astype(BF)

    gain = gain_ref[...]
    loads[0].wait()
    loads[1].wait()

    def query_step(i, carry):
        at = pl.ds(pl.multiple_of(i * 256, 256), 256)
        xn = (norm_rows(cand_v[at, :].astype(F32)) * gain).astype(BF)
        xn_v[at, :] = xn
        q_v[at, :] = silu(dot(xn, w_v[:, 2 * HD : 3 * HD])).astype(BF)
        return carry

    lax.fori_loop(0, 2, query_step, 0)

    tab_own[...] = jnp.zeros_like(tab_own)
    tab_sib[...] = jnp.zeros_like(tab_sib)
    for m, tab in ((1, tab_sib), (0, tab_own)):
        for s in range(CAP):
            first = (m * CAP + s) * CHIPS
            pick = pick_v[first : first + CHIPS, :]
            got = dot(pick, q_v[...])
            for h in range(HEADS):
                tab[pl.ds(c * 12 + h * CAP + s, CHIPS, stride=QROWS), :] = got[
                    :, h * HDIM : (h + 1) * HDIM
                ]
            tab[pl.ds(24 + c * CAP + s, CHIPS, stride=QROWS), :] = dot(pick, user_mat)
    sib_out[...] = tab_sib[...].astype(BF).reshape(CHIPS, QROWS, HDIM)

    pl.semaphore_wait(barrier, 23)
    swap = pltpu.make_async_remote_copy(
        src_ref=sib_out, dst_ref=sib_in, send_sem=sib_send, recv_sem=sib_recv,
        device_id=sibling, device_id_type=MESH,
    )
    swap.start()

    def say_ready(k, carry):
        pl.semaphore_signal(ready_sem, inc=1, device_id=plane_peer(k), device_id_type=MESH)
        return carry

    lax.fori_loop(1, 16, say_ready, 0)
    own = tab_own[...].astype(BF).reshape(CHIPS, QROWS, HDIM)
    msg[...] = own
    swap.wait()
    msg[...] = msg[...] + sib_in[...]
    pl.semaphore_wait(ready_sem, 15)

    land[0] = msg[0]

    def send_query(j, carry):
        grp = j // 32
        idx = grp * 32 + (j % 2) * 16 + (j % 32) // 2
        pltpu.make_async_remote_copy(
            src_ref=msg.at[idx], dst_ref=land.at[idx],
            send_sem=q_send.at[grp], recv_sem=q_recv.at[grp],
            device_id=peer(idx, 1), device_id_type=MESH,
        ).start()
        return carry

    lax.fori_loop(1, CHIPS, send_query, 0)

    loads[2].wait()
    loads[3].wait()
    loads[5].wait()

    def encode_step(i, carry):
        at = pl.ds(pl.multiple_of(i * 256, 256), 256)
        xn = (norm_rows(hist_v[at, :].astype(F32)) * gain).astype(BF)
        row = lax.broadcasted_iota(jnp.int32, (256, HD), 0)
        live = row < jnp.where(
            row < ROWS, len_ref[2 * i] * PIECE, len_ref[2 * i + 1] * PIECE + ROWS
        )
        keys = silu(dot(xn, w_v[:, 3 * HD :]))
        kv_v[at, :HD] = jnp.where(live, keys, 0.0).astype(BF)
        values = silu(dot(xn, w_v[:, HD : 2 * HD]))
        kv_v[at, HD:] = jnp.where(live, values, 0.0).astype(BF)
        pltpu.make_async_copy(kv_v.at[at, :], kv_hbm.at[at, :], kv_sem).start()
        return carry

    lax.fori_loop(0, USERS // 2, encode_step, 0)

    def remote_span(grp, ref, sem):
        return pltpu.make_async_copy(
            ref.at[pl.ds(grp * GSIZE, GSIZE)], ref.at[pl.ds(grp * GSIZE, GSIZE)], sem.at[grp]
        )

    def first_span(ref, sem):
        return pltpu.make_async_copy(
            ref.at[pl.ds(1, GSIZE - 1)], ref.at[pl.ds(1, GSIZE - 1)], sem.at[0]
        )

    half_scale = 0.5 * HDIM**-0.5

    def attend_group(grp):
        land_f[...] = land[pl.ds(grp * GSIZE, GSIZE)].astype(F32).reshape(GSIZE * QROWS, HDIM)
        uid = jnp.concatenate(
            [land_f[pl.ds(24 + j, GSIZE, stride=QROWS), :] for j in range(2 * CAP)], axis=0
        )
        for h in range(HEADS):
            query = jnp.concatenate(
                [
                    land_f[pl.ds(cs * 12 + h * CAP + s, GSIZE, stride=QROWS), :]
                    for cs in range(2)
                    for s in range(CAP)
                ],
                axis=0,
            ).astype(BF)
            total = None
            for pair in range(USERS // 2):
                at = slice(pair * 256, pair * 256 + 256)
                score = dot_t(query, kv_v[at, h * HDIM : (h + 1) * HDIM]) * half_scale
                weight = score + score * jnp.tanh(score)
                mine = jnp.concatenate([uid == 2.0 * pair, uid == 2.0 * pair + 1.0], axis=1)
                weight = jnp.where(mine, weight, 0.0).astype(BF)
                part = dot(weight, kv_v[at, HD + h * HDIM : HD + (h + 1) * HDIM])
                total = part if total is None else total + part
            for j in range(2 * CAP):
                row = (j // CAP) * 12 + h * CAP + j % CAP
                ret_f[pl.ds(row, GSIZE, stride=RROWS), :] = total[j * GSIZE : (j + 1) * GSIZE, :]
        ret_msg[pl.ds(grp * GSIZE, GSIZE)] = ret_f[...].reshape(GSIZE, RROWS, HDIM).astype(BF)

    def send_back(j, carry):
        grp = j // 32
        idx = grp * 32 + (j % 2) * 16 + (j % 32) // 2
        pltpu.make_async_remote_copy(
            src_ref=ret_msg.at[idx], dst_ref=ret_land.at[idx],
            send_sem=r_send.at[grp], recv_sem=r_recv.at[grp],
            device_id=peer(idx, -1), device_id_type=MESH,
        ).start()
        return carry

    first_span(land, q_recv).wait()
    attend_group(0)
    ret_land[0] = ret_msg[0]
    lax.fori_loop(1, 32, send_back, 0)

    def group_step(grp, carry):
        remote_span(grp, land, q_recv).wait()
        attend_group(grp)
        lax.fori_loop(grp * 32, grp * 32 + 32, send_back, 0)
        return carry

    lax.fori_loop(1, GROUPS, group_step, 0)

    loads[4].wait()

    def own_step(i, carry):
        at = pl.ds(pl.multiple_of(i * 256, 256), 256)
        xn = xn_v[at, :]
        u_v[at, :] = silu(dot(xn, w_v[:, :HD])).astype(BF)
        own_v = silu(dot(xn, w_v[:, HD : 2 * HD])).astype(BF).astype(F32)
        own_k = silu(dot(xn, w_v[:, 3 * HD :])).astype(BF).astype(F32)
        prod = q_v[at, :].astype(F32) * own_k
        for h in range(HEADS):
            lanes = slice(h * HDIM, (h + 1) * HDIM)
            score = jnp.sum(prod[:, lanes], axis=-1, keepdims=True) * half_scale
            weight = (score + score * jnp.tanh(score)).astype(BF).astype(F32)
            self_v[at, lanes] = weight * own_v[:, lanes]
        return carry

    lax.fori_loop(0, 2, own_step, 0)

    def hand_on(grp):
        span = pl.ds(grp * GSIZE, GSIZE)
        return pltpu.make_async_remote_copy(
            src_ref=ret_land.at[span], dst_ref=ret_sib.at[span],
            send_sem=f_send.at[grp], recv_sem=f_recv.at[grp],
            device_id=sibling, device_id_type=MESH,
        )

    first_span(ret_land, r_recv).wait()
    hand_on(0).start()

    def hand_step(grp, carry):
        remote_span(grp, ret_land, r_recv).wait()
        hand_on(grp).start()
        return carry

    lax.fori_loop(1, GROUPS, hand_step, 0)
    back_own[...] = ret_land[...].astype(F32).reshape(CHIPS * RROWS, HDIM)

    def hand_wait(grp, carry):
        hand_on(grp).wait()
        return carry

    lax.fori_loop(0, GROUPS, hand_wait, 0)
    back_sib[...] = ret_sib[...].astype(F32).reshape(CHIPS * RROWS, HDIM)
    for m, back in ((0, back_own), (1, back_sib)):
        for s in range(CAP):
            first = (m * CAP + s) * CHIPS
            for h in range(HEADS):
                back_v[first : first + CHIPS, h * HDIM : (h + 1) * HDIM] = back[
                    pl.ds(c * 12 + h * CAP + s, CHIPS, stride=RROWS), :
                ].astype(BF)

    def out_step(i, carry):
        at = pl.ds(pl.multiple_of(i * 256, 256), 256)
        attended = dot(place_v[at, :], back_v[...]) + self_v[at, :]
        normed = norm_rows(attended).astype(BF).astype(F32)
        out_ref[at, :] = (normed * u_v[at, :].astype(F32)).astype(BF)
        return carry

    lax.fori_loop(0, 2, out_step, 0)

    first_span(msg, q_send).wait()
    first_span(ret_msg, r_send).wait()

    def sent(grp, carry):
        remote_span(grp, msg, q_send).wait()
        remote_span(grp, ret_msg, r_send).wait()
        return carry

    lax.fori_loop(1, GROUPS, sent, 0)
    pltpu.make_async_copy(kv_v, kv_hbm, kv_sem).wait()


def body(history, hist_len, cand, cand_owner, cand_user, norm_gain, w_proj):
    any_spec = pl.BlockSpec(memory_space=pl.ANY)
    vmem = pl.BlockSpec(memory_space=pltpu.VMEM)
    dma = pltpu.SemaphoreType.DMA
    kv, out = pl.pallas_call(
        kernel,
        out_shape=(
            jax.ShapeDtypeStruct((USERS * ROWS, 2 * HD), BF),
            jax.ShapeDtypeStruct((CAND, HD), BF),
        ),
        in_specs=[
            pl.BlockSpec(memory_space=pltpu.SMEM), vmem, vmem, vmem, any_spec, any_spec, any_spec,
        ],
        out_specs=(any_spec, vmem),
        scratch_shapes=[
            pltpu.VMEM((CAND, D), BF),
            pltpu.VMEM((USERS * ROWS, D), BF),
            pltpu.VMEM((D, 4 * HD), BF),
            pltpu.VMEM((USERS * ROWS, 2 * HD), BF),
            pltpu.VMEM((CAND, D), BF),
            pltpu.VMEM((CAND, HD), BF),
            pltpu.VMEM((CAND, HD), BF),
            pltpu.VMEM((CAND, HD), F32),
            pltpu.VMEM((2 * CAP * CHIPS, CAND), BF),
            pltpu.VMEM((CAND, 2 * CAP * CHIPS), BF),
            pltpu.VMEM((CHIPS * QROWS, HDIM), F32),
            pltpu.VMEM((CHIPS * QROWS, HDIM), F32),
            pltpu.VMEM((CHIPS, QROWS, HDIM), BF),
            pltpu.VMEM((CHIPS, QROWS, HDIM), BF),
            pltpu.VMEM((CHIPS, QROWS, HDIM), BF),
            pltpu.VMEM((CHIPS, QROWS, HDIM), BF),
            pltpu.VMEM((GSIZE * QROWS, HDIM), F32),
            pltpu.VMEM((GSIZE * RROWS, HDIM), F32),
            pltpu.VMEM((CHIPS, RROWS, HDIM), BF),
            pltpu.VMEM((CHIPS, RROWS, HDIM), BF),
            pltpu.VMEM((CHIPS, RROWS, HDIM), BF),
            pltpu.VMEM((CHIPS * RROWS, HDIM), F32),
            pltpu.VMEM((CHIPS * RROWS, HDIM), F32),
            pltpu.VMEM((2 * CAP * CHIPS, HD), BF),
            dma((6,)),
            dma,
            dma,
            dma,
            pltpu.SemaphoreType.REGULAR,
            dma((GROUPS,)),
            dma((GROUPS,)),
            dma((GROUPS,)),
            dma((GROUPS,)),
            dma((GROUPS,)),
            dma((GROUPS,)),
        ],
        compiler_params=pltpu.CompilerParams(
            collective_id=0, has_side_effects=True, vmem_limit_bytes=56 << 20
        ),
        cost_estimate=pl.CostEstimate(
            flops=12_000_000_000, bytes_accessed=12_000_000, transcendentals=8_000_000
        ),
        name="routed_attention",
    )(
        hist_len,
        cand_owner,
        cand_user.reshape(1, CAND),
        norm_gain.reshape(1, D),
        cand,
        history.reshape(USERS * ROWS, D),
        w_proj,
    )
    return kv.reshape(USERS, ROWS, 2 * HD), out


def solution(mesh):
    placed = (
        P(("grp", "enc"), None, None),
        P(("grp", "enc")),
        P(("grp", "enc"), None),
        P(("grp", "enc"), None),
        P(("grp", "enc")),
        P(),
        P(),
    )
    return jax.shard_map(
        body,
        mesh=mesh,
        in_specs=placed,
        out_specs=(P(("grp", "enc"), None, None), P(("grp", "enc"), None)),
        check_vma=False,
    )
```

```python
import functools

import jax
import jax.numpy as jnp
from jax import lax
from jax.experimental import pallas as pl
from jax.experimental.pallas import tpu as pltpu
from jax.sharding import PartitionSpec as P

MESH = pl.DeviceIdType.MESH
HDIM = 128
HEADS = 4
HD = 512
D = 1024
PIECE = 64
ROWS = 128
USERS = 12
CAND = 512
CAP = 3
CHIPS = 128
GROUPS = 4
GSIZE = 32
MROWS = 24
BF = jnp.bfloat16
F32 = jnp.float32


def silu(x):
    half = 0.5 * x
    return half + half * jnp.tanh(half)


def norm_rows(x):
    center = x - jnp.mean(x, axis=-1, keepdims=True)
    spread = jnp.mean(center * center, axis=-1, keepdims=True)
    return center * lax.rsqrt(spread + 1e-5)


def dot(a, b):
    return jnp.dot(a, b, preferred_element_type=F32)


def dot_t(a, b):
    return lax.dot_general(a, b, (((1,), (1,)), ((), ())), preferred_element_type=F32)


def kernel(
    len_ref, owner_ref, user_ref, gain_ref, cand_hbm, hist_hbm, w_hbm,
    kv_hbm, out_ref,
    cand_v, hist_v, w_v, kv_v, xn_v, q_v, u_v, att_v, place_v,
    sib_out, sib_in, tab, msg, land, land_f, ret_f, ret_msg, ret_land, ret_sib, back_f, back_v,
    slot_out, slot_in, ring_out, ring_in, plane_out, plane_in,
    load_sem, kv_sem, sib_send, sib_recv, ready_sem,
    q_send, q_recv, r_send, r_recv, f_send, f_recv, s_send, s_recv,
):
    g, e = lax.axis_index("grp"), lax.axis_index("enc")
    y, x, c = e // 8, (e // 2) % 4, e % 2
    sibling = (g, y * 8 + x * 2 + 1 - c)

    def plane_peer(k):
        return g, ((y + k // 4) % 4) * 8 + ((x + k % 4) % 4) * 2 + c

    def ring_shift(r):
        return (1 - r % 2) * ((4 - r // 2) % 4) + (r % 2) * (4 + r // 2)

    def peer(idx, sign):
        dz, k = ring_shift(idx // 16), idx % 16
        py = (y + sign * (k // 4) + 4) % 4
        px = (x + sign * (k % 4) + 4) % 4
        return (g + sign * dz + 8) % 8, py * 8 + px * 2 + c

    cols = [(2 * HD, 3 * HD), (3 * HD, 4 * HD), (HD, 2 * HD), (0, HD)]
    loads = [pltpu.make_async_copy(cand_hbm, cand_v, load_sem.at[0])]
    for i, (lo, hi) in enumerate(cols):
        loads.append(
            pltpu.make_async_copy(
                w_hbm.at[:, pl.ds(lo, HD)], w_v.at[:, pl.ds(lo, HD)], load_sem.at[1 + i]
            )
        )
    loads.append(pltpu.make_async_copy(hist_hbm, hist_v, load_sem.at[5]))
    for i in (0, 1, 5, 2, 3, 4):
        loads[i].start()

    barrier = pltpu.get_barrier_semaphore()

    def greet_ring(k, carry):
        pl.semaphore_signal(
            barrier, inc=1, device_id=((g + k) % 8, e), device_id_type=MESH
        )
        return carry

    def greet_plane(k, carry):
        pl.semaphore_signal(barrier, inc=1, device_id=plane_peer(k), device_id_type=MESH)
        return carry

    lax.fori_loop(1, 8, greet_ring, 0)
    lax.fori_loop(1, 16, greet_plane, 0)
    pl.semaphore_signal(barrier, inc=1, device_id=sibling, device_id_type=MESH)

    rows_i = lax.broadcasted_iota(jnp.int32, (CAND, CAND), 0)
    cols_i = lax.broadcasted_iota(jnp.int32, (CAND, CAND), 1)
    owner = owner_ref[...]
    owner_f = owner.astype(F32)
    owner_col = jnp.sum(jnp.where(rows_i == cols_i, owner_f, 0.0), axis=1, keepdims=True)
    same = (owner_col == owner_f) & (rows_i < cols_i)
    rank = jnp.sum(jnp.where(same, 1.0, 0.0), axis=0, keepdims=True).astype(jnp.int32)
    to_g, to_e = owner // 32, owner % 32
    dz = (to_g - g + 8) % 8
    half = dz // 4
    grp = jnp.where(half == 1, dz - 4, (4 - dz) % 4)
    ry = (to_e // 8 - y + 4) % 4
    rx = ((to_e // 2) % 4 - x + 4) % 4
    other = jnp.where(to_e % 2 == c, 0, 1)
    shift = ry * 4 + rx
    code = (other * CAP + rank) * CHIPS + grp * 32 + half * 16 + shift

    def pick(j):
        slot = lax.broadcasted_iota(jnp.int32, (CHIPS, CAND), 0) + j * CHIPS
        return jnp.where(slot == code, 1.0, 0.0).astype(BF)

    ring_row = lax.broadcasted_iota(jnp.int32, (8, CAND), 0) + 8 * other
    slot_lane = lax.broadcasted_iota(jnp.int32, (HDIM, CAND), 0)
    lane_hot = jnp.where(slot_lane == (c * CAP + rank) * 16 + shift, 1.0, 0.0).astype(BF)
    user_f = user_ref[...].astype(F32)

    def slot_users(m):
        mine = ring_row == grp * 2 + half + 8 * m
        return dot_t(jnp.where(mine, user_f, 0.0).astype(BF), lane_hot)

    slot_out[...] = slot_users(1)

    gain = gain_ref[...]
    loads[0].wait()
    loads[1].wait()

    def query_step(i, carry):
        at = pl.ds(pl.multiple_of(i * 256, 256), 256)
        xn = (norm_rows(cand_v[at, :].astype(F32)) * gain).astype(BF)
        xn_v[at, :] = xn
        q_v[at, :] = silu(dot(xn, w_v[:, 2 * HD : 3 * HD])).astype(BF)
        return carry

    lax.fori_loop(0, 2, query_step, 0)

    def swap(s):
        return pltpu.make_async_remote_copy(
            src_ref=sib_out.at[s], dst_ref=sib_in.at[s],
            send_sem=sib_send.at[s], recv_sem=sib_recv.at[s],
            device_id=sibling, device_id_type=MESH,
        )

    swap_users = pltpu.make_async_remote_copy(
        src_ref=slot_out, dst_ref=slot_in, send_sem=sib_send.at[CAP], recv_sem=sib_recv.at[CAP],
        device_id=sibling, device_id_type=MESH,
    )

    for s in range(CAP):
        sib_out[s] = dot(pick(CAP + s), q_v[...]).astype(BF)
        if s == 0:
            pl.semaphore_wait(barrier, 23)
            swap_users.start()
        swap(s).start()

    def say_ready(k, carry):
        pl.semaphore_signal(ready_sem, inc=1, device_id=plane_peer(k), device_id_type=MESH)
        return carry

    lax.fori_loop(1, 16, say_ready, 0)

    def lay(rows, core, s):
        for h in range(HEADS):
            tab[pl.ds(core * 12 + h * CAP + s, CHIPS, stride=MROWS), :] = rows[
                :, h * HDIM : (h + 1) * HDIM
            ]

    for s in range(CAP):
        lay(dot(pick(s), q_v[...]), c, s)
    own_users = slot_users(0)
    for s in range(CAP):
        swap(s).wait()
        lay(sib_in[s].astype(F32), 1 - c, s)
    pl.semaphore_wait(ready_sem, 15)

    def send_query(j, carry):
        idx = (j // 32) * 32 + (j % 2) * 16 + (j % 32) // 2
        pltpu.make_async_remote_copy(
            src_ref=msg.at[idx], dst_ref=land.at[idx],
            send_sem=q_send.at[j // 32], recv_sem=q_recv.at[j // 32],
            device_id=peer(idx, 1), device_id_type=MESH,
        ).start()
        return carry

    def fill(grp):
        rows = pl.ds(grp * GSIZE * MROWS, GSIZE * MROWS)
        msg[pl.ds(grp * GSIZE, GSIZE)] = tab[rows, :].reshape(GSIZE, MROWS, HDIM).astype(BF)

    def send_group(grp):
        lax.fori_loop(grp * GSIZE, grp * GSIZE + GSIZE, send_query, 0)

    fill(0)
    lax.fori_loop(1, GSIZE, send_query, 0)
    fill(1)
    send_group(1)
    land[0] = msg[0]
    fill(2)
    fill(3)

    def remote_span(grp, ref, sem):
        return pltpu.make_async_copy(
            ref.at[pl.ds(grp * GSIZE, GSIZE)], ref.at[pl.ds(grp * GSIZE, GSIZE)], sem.at[grp]
        )

    def first_span(ref, sem):
        return pltpu.make_async_copy(
            ref.at[pl.ds(1, GSIZE - 1)], ref.at[pl.ds(1, GSIZE - 1)], sem.at[0]
        )

    swap_users.wait()
    ring_out[...] = (own_users + slot_in[...]).reshape(8, 1, HDIM)
    ring_in[0] = ring_out[0]

    def send_ring(r, carry):
        pltpu.make_async_remote_copy(
            src_ref=ring_out.at[r], dst_ref=ring_in.at[r],
            send_sem=s_send.at[0], recv_sem=s_recv.at[0],
            device_id=((g + ring_shift(r)) % 8, e), device_id_type=MESH,
        ).start()
        return carry

    lax.fori_loop(1, 8, send_ring, 0)

    loads[2].wait()
    loads[3].wait()
    loads[5].wait()

    def encode_step(i, carry):
        at = pl.ds(pl.multiple_of(i * 256, 256), 256)
        xn = (norm_rows(hist_v[at, :].astype(F32)) * gain).astype(BF)
        row = lax.broadcasted_iota(jnp.int32, (256, HD), 0)
        live = row < jnp.where(
            row < ROWS, len_ref[2 * i] * PIECE, len_ref[2 * i + 1] * PIECE + ROWS
        )
        keys = silu(dot(xn, w_v[:, 3 * HD :]))
        kv_v[at, :HD] = jnp.where(live, keys, 0.0).astype(BF)
        values = silu(dot(xn, w_v[:, HD : 2 * HD]))
        kv_v[at, HD:] = jnp.where(live, values, 0.0).astype(BF)
        pltpu.make_async_copy(kv_v.at[at, :], kv_hbm.at[at, :], kv_sem).start()
        return carry

    lax.fori_loop(0, 2, encode_step, 0)
    first_span(msg, q_send).wait()
    send_group(2)
    lax.fori_loop(2, 4, encode_step, 0)
    remote_span(1, msg, q_send).wait()
    send_group(3)

    ring_rest = pl.ds(1, 7)
    pltpu.make_async_copy(ring_in.at[ring_rest], ring_in.at[ring_rest], s_recv.at[0]).wait()
    plane_out[...] = ring_in[...].reshape(8, HDIM)
    plane_in[0:8, :] = plane_out[...]

    def send_plane(k, carry):
        pltpu.make_async_remote_copy(
            src_ref=plane_out, dst_ref=plane_in.at[pl.ds(k * 8, 8), :],
            send_sem=s_send.at[1], recv_sem=s_recv.at[1],
            device_id=plane_peer(k), device_id_type=MESH,
        ).start()
        return carry

    lax.fori_loop(1, 16, send_plane, 0)
    lax.fori_loop(4, 6, encode_step, 0)
    plane_rest = plane_in.at[pl.ds(8, 120), :]
    pltpu.make_async_copy(plane_rest, plane_rest, s_recv.at[1]).wait()

    half_scale = 0.5 * HDIM**-0.5

    def attend_group(grp):
        land_f[...] = land[pl.ds(grp * GSIZE, GSIZE)].astype(F32).reshape(GSIZE * MROWS, HDIM)
        lane = lax.broadcasted_iota(jnp.int32, (16, HDIM), 1)
        row = lax.broadcasted_iota(jnp.int32, (16, HDIM), 0)
        known = [plane_in[pl.ds(2 * grp + part, 16, stride=8), :] for part in range(2)]
        uid = jnp.concatenate(
            [
                jnp.broadcast_to(
                    jnp.sum(
                        jnp.where(lane == row + 16 * j, known[part], 0.0), axis=1, keepdims=True
                    ),
                    (16, HDIM),
                )
                for j in range(2 * CAP)
                for part in range(2)
            ],
            axis=0,
        )
        for h in range(HEADS):
            query = jnp.concatenate(
                [
                    land_f[pl.ds(cs * 12 + h * CAP + s, GSIZE, stride=MROWS), :]
                    for cs in range(2)
                    for s in range(CAP)
                ],
                axis=0,
            ).astype(BF)
            total = None
            for pair in range(USERS // 2):
                at = slice(pair * 256, pair * 256 + 256)
                score = dot_t(query, kv_v[at, h * HDIM : (h + 1) * HDIM]) * half_scale
                weight = score + score * jnp.tanh(score)
                mine = jnp.concatenate([uid == 2.0 * pair, uid == 2.0 * pair + 1.0], axis=1)
                weight = jnp.where(mine, weight, 0.0).astype(BF)
                part = dot(weight, kv_v[at, HD + h * HDIM : HD + (h + 1) * HDIM])
                total = part if total is None else total + part
            for j in range(2 * CAP):
                row_at = (j // CAP) * 12 + h * CAP + j % CAP
                ret_f[pl.ds(row_at, GSIZE, stride=MROWS), :] = total[
                    j * GSIZE : (j + 1) * GSIZE, :
                ]
        ret_msg[pl.ds(grp * GSIZE, GSIZE)] = ret_f[...].reshape(GSIZE, MROWS, HDIM).astype(BF)

    def send_back(j, carry):
        idx = (j // 32) * 32 + (j % 2) * 16 + (j % 32) // 2
        pltpu.make_async_remote_copy(
            src_ref=ret_msg.at[idx], dst_ref=ret_land.at[idx],
            send_sem=r_send.at[j // 32], recv_sem=r_recv.at[j // 32],
            device_id=peer(idx, -1), device_id_type=MESH,
        ).start()
        return carry

    first_span(land, q_recv).wait()
    attend_group(0)
    ret_land[0] = ret_msg[0]
    lax.fori_loop(1, GSIZE, send_back, 0)

    def group_step(grp, carry):
        remote_span(grp, land, q_recv).wait()
        attend_group(grp)
        lax.fori_loop(grp * GSIZE, grp * GSIZE + GSIZE, send_back, 0)
        return carry

    lax.fori_loop(1, GROUPS, group_step, 0)

    loads[4].wait()

    def own_step(i, carry):
        at = pl.ds(pl.multiple_of(i * 256, 256), 256)
        xn = xn_v[at, :]
        u_v[at, :] = silu(dot(xn, w_v[:, :HD])).astype(BF)
        own_v = silu(dot(xn, w_v[:, HD : 2 * HD])).astype(BF).astype(F32)
        own_k = silu(dot(xn, w_v[:, 3 * HD :])).astype(BF).astype(F32)
        prod = q_v[at, :].astype(F32) * own_k
        for h in range(HEADS):
            lanes = slice(h * HDIM, (h + 1) * HDIM)
            score = jnp.sum(prod[:, lanes], axis=-1, keepdims=True) * half_scale
            weight = (score + score * jnp.tanh(score)).astype(BF).astype(F32)
            att_v[at, lanes] = weight * own_v[:, lanes]
        return carry

    lax.fori_loop(0, 2, own_step, 0)
    place = (grp * 256 + (other * CAP + rank) * 32 + half * 16 + shift).astype(F32)
    place_col = jnp.sum(jnp.where(rows_i == cols_i, place, 0.0), axis=1, keepdims=True)
    lane_slot = lax.broadcasted_iota(jnp.int32, (CAND, GROUPS * 256), 1).astype(F32)
    place_v[...] = jnp.where(lane_slot == place_col, 1.0, 0.0).astype(BF)
    back_v[192:, :] = jnp.zeros((64, HD), BF)

    def hand_on(grp):
        span = pl.ds(grp * GSIZE, GSIZE)
        return pltpu.make_async_remote_copy(
            src_ref=ret_land.at[span], dst_ref=ret_sib.at[span],
            send_sem=f_send.at[grp], recv_sem=f_recv.at[grp],
            device_id=sibling, device_id_type=MESH,
        )

    def unpack(ref, grp, m):
        back_f[...] = ref[pl.ds(grp * GSIZE, GSIZE)].astype(F32).reshape(GSIZE * MROWS, HDIM)
        for s in range(CAP):
            first = (m * CAP + s) * GSIZE
            for h in range(HEADS):
                back_v[first : first + GSIZE, h * HDIM : (h + 1) * HDIM] = back_f[
                    pl.ds(c * 12 + h * CAP + s, GSIZE, stride=MROWS), :
                ].astype(BF)

    def take(grp):
        hand_on(grp).start()
        unpack(ret_land, grp, 0)
        hand_on(grp).wait()
        unpack(ret_sib, grp, 1)

    def gather(grp):
        def gather_step(i, carry):
            at = pl.ds(pl.multiple_of(i * 256, 256), 256)
            slots = pl.ds(pl.multiple_of(grp * 256, 256), 256)
            att_v[at, :] += dot(place_v[at, slots], back_v[...])
            return carry

        lax.fori_loop(0, 2, gather_step, 0)

    first_span(ret_land, r_recv).wait()
    take(0)
    gather(0)

    def take_step(grp, carry):
        remote_span(grp, ret_land, r_recv).wait()
        take(grp)
        gather(grp)
        return carry

    lax.fori_loop(1, GROUPS - 1, take_step, 0)
    remote_span(GROUPS - 1, ret_land, r_recv).wait()
    take(GROUPS - 1)

    def out_step(i, carry):
        at = pl.ds(pl.multiple_of(i * 256, 256), 256)
        last = dot(place_v[at, (GROUPS - 1) * 256 :], back_v[...])
        normed = norm_rows(att_v[at, :] + last).astype(BF).astype(F32)
        out_ref[at, :] = (normed * u_v[at, :].astype(F32)).astype(BF)
        return carry

    lax.fori_loop(0, 2, out_step, 0)

    remote_span(2, msg, q_send).wait()
    remote_span(3, msg, q_send).wait()
    first_span(ret_msg, r_send).wait()

    def sent(grp, carry):
        remote_span(grp, ret_msg, r_send).wait()
        return carry

    lax.fori_loop(1, GROUPS, sent, 0)
    pltpu.make_async_copy(ring_out.at[ring_rest], ring_out.at[ring_rest], s_send.at[0]).wait()
    pltpu.make_async_copy(plane_rest, plane_rest, s_send.at[1]).wait()
    pltpu.make_async_copy(kv_v, kv_hbm, kv_sem).wait()


def write_out(kv_ref, rows_ref, kv_out, rows_out, kv_v, rows_v, in_sem, out_sem):
    spans = [pl.ds(i * 192, 192) for i in range(8)]
    takes = [
        pltpu.make_async_copy(kv_ref.at[span, :], kv_v.at[span, :], in_sem.at[i])
        for i, span in enumerate(spans)
    ]
    puts = [
        pltpu.make_async_copy(kv_v.at[span, :], kv_out.at[span, :], out_sem.at[i])
        for i, span in enumerate(spans)
    ]
    takes.append(pltpu.make_async_copy(rows_ref, rows_v, in_sem.at[8]))
    puts.append(pltpu.make_async_copy(rows_v, rows_out, out_sem.at[8]))
    for take in takes:
        take.start()
    for take, put in zip(takes, puts):
        take.wait()
        put.start()
    for put in puts:
        put.wait()


def body(history, hist_len, cand, cand_owner, cand_user, norm_gain, w_proj):
    any_spec = pl.BlockSpec(memory_space=pl.ANY)
    vmem = pl.BlockSpec(memory_space=pltpu.VMEM)
    dma = pltpu.SemaphoreType.DMA
    results = (
        jax.ShapeDtypeStruct((USERS * ROWS, 2 * HD), BF),
        jax.ShapeDtypeStruct((CAND, HD), BF),
    )
    kv, out = pl.pallas_call(
        kernel,
        out_shape=results,
        in_specs=[
            pl.BlockSpec(memory_space=pltpu.SMEM), vmem, vmem, vmem, any_spec, any_spec, any_spec,
        ],
        out_specs=(any_spec, vmem),
        scratch_shapes=[
            pltpu.VMEM((CAND, D), BF),
            pltpu.VMEM((USERS * ROWS, D), BF),
            pltpu.VMEM((D, 4 * HD), BF),
            pltpu.VMEM((USERS * ROWS, 2 * HD), BF),
            pltpu.VMEM((CAND, D), BF),
            pltpu.VMEM((CAND, HD), BF),
            pltpu.VMEM((CAND, HD), BF),
            pltpu.VMEM((CAND, HD), F32),
            pltpu.VMEM((CAND, GROUPS * 256), BF),
            pltpu.VMEM((CAP, CHIPS, HD), BF),
            pltpu.VMEM((CAP, CHIPS, HD), BF),
            pltpu.VMEM((CHIPS * MROWS, HDIM), F32),
            pltpu.VMEM((CHIPS, MROWS, HDIM), BF),
            pltpu.VMEM((CHIPS, MROWS, HDIM), BF),
            pltpu.VMEM((GSIZE * MROWS, HDIM), F32),
            pltpu.VMEM((GSIZE * MROWS, HDIM), F32),
            pltpu.VMEM((CHIPS, MROWS, HDIM), BF),
            pltpu.VMEM((CHIPS, MROWS, HDIM), BF),
            pltpu.VMEM((CHIPS, MROWS, HDIM), BF),
            pltpu.VMEM((GSIZE * MROWS, HDIM), F32),
            pltpu.VMEM((256, HD), BF),
            pltpu.VMEM((8, HDIM), F32),
            pltpu.VMEM((8, HDIM), F32),
            pltpu.VMEM((8, 1, HDIM), F32),
            pltpu.VMEM((8, 1, HDIM), F32),
            pltpu.VMEM((8, HDIM), F32),
            pltpu.VMEM((HDIM, HDIM), F32),
            dma((6,)),
            dma,
            dma((CAP + 1,)),
            dma((CAP + 1,)),
            pltpu.SemaphoreType.REGULAR,
            dma((GROUPS,)),
            dma((GROUPS,)),
            dma((GROUPS,)),
            dma((GROUPS,)),
            dma((GROUPS,)),
            dma((GROUPS,)),
            dma((2,)),
            dma((2,)),
        ],
        compiler_params=pltpu.CompilerParams(
            collective_id=0, has_side_effects=True, vmem_limit_bytes=56 << 20
        ),
        cost_estimate=pl.CostEstimate(
            flops=12_000_000_000, bytes_accessed=12_000_000, transcendentals=8_000_000
        ),
        name="routed_attention",
    )(
        hist_len,
        cand_owner.reshape(1, CAND),
        cand_user.reshape(1, CAND),
        norm_gain.reshape(1, D),
        cand,
        history.reshape(USERS * ROWS, D),
        w_proj,
    )
    kv, out = pl.pallas_call(
        write_out,
        out_shape=results,
        in_specs=[any_spec, any_spec],
        out_specs=(any_spec, any_spec),
        scratch_shapes=[
            pltpu.VMEM((USERS * ROWS, 2 * HD), BF), pltpu.VMEM((CAND, HD), BF), dma((9,)), dma((9,)),
        ],
        name="write_out",
    )(kv, out)
    return kv.reshape(USERS, ROWS, 2 * HD), out


def solution(mesh):
    placed = (
        P(("grp", "enc"), None, None),
        P(("grp", "enc")),
        P(("grp", "enc"), None),
        P(("grp", "enc"), None),
        P(("grp", "enc")),
        P(),
        P(),
    )
    return jax.shard_map(
        body,
        mesh=mesh,
        in_specs=placed,
        out_specs=(P(("grp", "enc"), None, None), P(("grp", "enc"), None)),
        check_vma=False,
    )
```

```python
import functools

import jax
import jax.numpy as jnp
from jax import lax
from jax.experimental import pallas as pl
from jax.experimental.pallas import tpu as pltpu
from jax.sharding import PartitionSpec as P

MESH = pl.DeviceIdType.MESH
HDIM = 128
HEADS = 4
HD = 512
D = 1024
PIECE = 64
ROWS = 128
USERS = 12
CAND = 512
CAP = 3
CHIPS = 128
GROUPS = 4
GSIZE = 32
MROWS = 24
BF = jnp.bfloat16
F32 = jnp.float32


def silu(x):
    half = 0.5 * x
    return half + half * jnp.tanh(half)


def norm_rows(x):
    center = x - jnp.mean(x, axis=-1, keepdims=True)
    spread = jnp.mean(center * center, axis=-1, keepdims=True)
    return center * lax.rsqrt(spread + 1e-5)


def dot(a, b):
    return jnp.dot(a, b, preferred_element_type=F32)


def dot_t(a, b):
    return lax.dot_general(a, b, (((1,), (1,)), ((), ())), preferred_element_type=F32)


def kernel(
    len_ref, owner_ref, user_ref, gain_ref, cand_hbm, hist_hbm, w_hbm,
    kv_hbm, out_ref,
    cand_v, hist_v, w_v, kv_v, xn_v, q_v, u_v, att_v, place_v,
    sib_out, sib_in, tab, msg, land, land_f, ret_f, ret_msg, ret_land, ret_sib, back_f, back_v,
    slot_out, slot_in, ring_out, ring_in, plane_out, plane_in,
    load_sem, kv_sem, sib_send, sib_recv, ready_sem,
    q_send, q_recv, r_send, r_recv, f_send, f_recv, s_send, s_recv,
):
    g, e = lax.axis_index("grp"), lax.axis_index("enc")
    y, x, c = e // 8, (e // 2) % 4, e % 2
    sibling = (g, y * 8 + x * 2 + 1 - c)

    def plane_peer(k):
        return g, ((y + k // 4) % 4) * 8 + ((x + k % 4) % 4) * 2 + c

    def ring_shift(r):
        return (1 - r % 2) * ((4 - r // 2) % 4) + (r % 2) * (4 + r // 2)

    def peer(idx, sign):
        dz, k = ring_shift(idx // 16), idx % 16
        py = (y + sign * (k // 4) + 4) % 4
        px = (x + sign * (k % 4) + 4) % 4
        return (g + sign * dz + 8) % 8, py * 8 + px * 2 + c

    cols = [(2 * HD, 3 * HD), (3 * HD, 4 * HD), (HD, 2 * HD), (0, HD)]
    loads = [pltpu.make_async_copy(cand_hbm, cand_v, load_sem.at[0])]
    for i, (lo, hi) in enumerate(cols):
        loads.append(
            pltpu.make_async_copy(
                w_hbm.at[:, pl.ds(lo, HD)], w_v.at[:, pl.ds(lo, HD)], load_sem.at[1 + i]
            )
        )
    loads.append(pltpu.make_async_copy(hist_hbm, hist_v, load_sem.at[5]))
    for i in (0, 1, 5, 2, 3, 4):
        loads[i].start()

    barrier = pltpu.get_barrier_semaphore()

    def greet_ring(k, carry):
        pl.semaphore_signal(
            barrier, inc=1, device_id=((g + k) % 8, e), device_id_type=MESH
        )
        return carry

    def greet_plane(k, carry):
        pl.semaphore_signal(barrier, inc=1, device_id=plane_peer(k), device_id_type=MESH)
        return carry

    lax.fori_loop(1, 8, greet_ring, 0)
    lax.fori_loop(1, 16, greet_plane, 0)
    pl.semaphore_signal(barrier, inc=1, device_id=sibling, device_id_type=MESH)

    rows_i = lax.broadcasted_iota(jnp.int32, (CAND, CAND), 0)
    cols_i = lax.broadcasted_iota(jnp.int32, (CAND, CAND), 1)
    owner = owner_ref[...]
    owner_f = owner.astype(F32)
    owner_col = jnp.sum(jnp.where(rows_i == cols_i, owner_f, 0.0), axis=1, keepdims=True)
    same = (owner_col == owner_f) & (rows_i < cols_i)
    rank = jnp.sum(jnp.where(same, 1.0, 0.0), axis=0, keepdims=True).astype(jnp.int32)
    to_g, to_e = owner // 32, owner % 32
    dz = (to_g - g + 8) % 8
    half = dz // 4
    grp = jnp.where(half == 1, dz - 4, (4 - dz) % 4)
    ry = (to_e // 8 - y + 4) % 4
    rx = ((to_e // 2) % 4 - x + 4) % 4
    other = jnp.where(to_e % 2 == c, 0, 1)
    shift = ry * 4 + rx
    code = (other * CAP + rank) * CHIPS + grp * 32 + half * 16 + shift

    def pick(j):
        slot = lax.broadcasted_iota(jnp.int32, (CHIPS, CAND), 0) + j * CHIPS
        return jnp.where(slot == code, 1.0, 0.0).astype(BF)

    ring_row = lax.broadcasted_iota(jnp.int32, (8, CAND), 0) + 8 * other
    slot_lane = lax.broadcasted_iota(jnp.int32, (HDIM, CAND), 0)
    lane_hot = jnp.where(slot_lane == (c * CAP + rank) * 16 + shift, 1.0, 0.0).astype(BF)
    user_f = user_ref[...].astype(F32)

    def slot_users(m):
        mine = ring_row == grp * 2 + half + 8 * m
        return dot_t(jnp.where(mine, user_f, 0.0).astype(BF), lane_hot)

    slot_out[...] = slot_users(1)

    gain = gain_ref[...]
    loads[0].wait()
    loads[1].wait()

    def query_step(i, carry):
        at = pl.ds(pl.multiple_of(i * 256, 256), 256)
        xn = (norm_rows(cand_v[at, :].astype(F32)) * gain).astype(BF)
        xn_v[at, :] = xn
        q_v[at, :] = silu(dot(xn, w_v[:, 2 * HD : 3 * HD])).astype(BF)
        return carry

    lax.fori_loop(0, 2, query_step, 0)

    def swap(s):
        return pltpu.make_async_remote_copy(
            src_ref=sib_out.at[s], dst_ref=sib_in.at[s],
            send_sem=sib_send.at[s], recv_sem=sib_recv.at[s],
            device_id=sibling, device_id_type=MESH,
        )

    swap_users = pltpu.make_async_remote_copy(
        src_ref=slot_out, dst_ref=slot_in, send_sem=sib_send.at[CAP], recv_sem=sib_recv.at[CAP],
        device_id=sibling, device_id_type=MESH,
    )

    for s in range(CAP):
        sib_out[s] = dot(pick(CAP + s), q_v[...]).astype(BF)
        if s == 0:
            pl.semaphore_wait(barrier, 23)
            swap_users.start()
        swap(s).start()

    def say_ready(k, carry):
        pl.semaphore_signal(ready_sem, inc=1, device_id=plane_peer(k), device_id_type=MESH)
        return carry

    lax.fori_loop(1, 16, say_ready, 0)

    def lay(rows, core, s):
        for h in range(HEADS):
            tab[pl.ds(core * 12 + h * CAP + s, CHIPS, stride=MROWS), :] = rows[
                :, h * HDIM : (h + 1) * HDIM
            ]

    for s in range(CAP):
        lay(dot(pick(s), q_v[...]), c, s)
    own_users = slot_users(0)
    swap_users.wait()
    ring_out[...] = (own_users + slot_in[...]).reshape(8, 1, HDIM)
    ring_in[0] = ring_out[0]

    def send_ring(r, carry):
        pltpu.make_async_remote_copy(
            src_ref=ring_out.at[r], dst_ref=ring_in.at[r],
            send_sem=s_send.at[0], recv_sem=s_recv.at[0],
            device_id=((g + ring_shift(r)) % 8, e), device_id_type=MESH,
        ).start()
        return carry

    lax.fori_loop(1, 8, send_ring, 0)

    for s in range(CAP):
        swap(s).wait()
        lay(sib_in[s].astype(F32), 1 - c, s)
    pl.semaphore_wait(ready_sem, 15)

    def send_query(j, carry):
        idx = (j // 32) * 32 + (j % 2) * 16 + (j % 32) // 2
        pltpu.make_async_remote_copy(
            src_ref=msg.at[idx], dst_ref=land.at[idx],
            send_sem=q_send.at[j // 32], recv_sem=q_recv.at[j // 32],
            device_id=peer(idx, 1), device_id_type=MESH,
        ).start()
        return carry

    def fill(grp):
        rows = pl.ds(grp * GSIZE * MROWS, GSIZE * MROWS)
        msg[pl.ds(grp * GSIZE, GSIZE)] = tab[rows, :].reshape(GSIZE, MROWS, HDIM).astype(BF)

    def send_group(grp):
        lax.fori_loop(grp * GSIZE, grp * GSIZE + GSIZE, send_query, 0)

    fill(0)
    lax.fori_loop(1, GSIZE, send_query, 0)
    fill(1)

    ring_rest = pl.ds(1, 7)
    pltpu.make_async_copy(ring_in.at[ring_rest], ring_in.at[ring_rest], s_recv.at[0]).wait()
    plane_out[...] = ring_in[...].reshape(8, HDIM)
    plane_in[0:8, :] = plane_out[...]

    def send_plane(k, carry):
        pltpu.make_async_remote_copy(
            src_ref=plane_out, dst_ref=plane_in.at[pl.ds(k * 8, 8), :],
            send_sem=s_send.at[1], recv_sem=s_recv.at[1],
            device_id=plane_peer(k), device_id_type=MESH,
        ).start()
        return carry

    lax.fori_loop(1, 16, send_plane, 0)

    send_group(1)
    land[0] = msg[0]
    fill(2)
    fill(3)

    def remote_span(grp, ref, sem):
        return pltpu.make_async_copy(
            ref.at[pl.ds(grp * GSIZE, GSIZE)], ref.at[pl.ds(grp * GSIZE, GSIZE)], sem.at[grp]
        )

    def first_span(ref, sem):
        return pltpu.make_async_copy(
            ref.at[pl.ds(1, GSIZE - 1)], ref.at[pl.ds(1, GSIZE - 1)], sem.at[0]
        )

    loads[2].wait()
    loads[3].wait()
    loads[5].wait()

    def encode_step(i, carry):
        at = pl.ds(pl.multiple_of(i * 256, 256), 256)
        xn = (norm_rows(hist_v[at, :].astype(F32)) * gain).astype(BF)
        row = lax.broadcasted_iota(jnp.int32, (256, HD), 0)
        live = row < jnp.where(
            row < ROWS, len_ref[2 * i] * PIECE, len_ref[2 * i + 1] * PIECE + ROWS
        )
        keys = silu(dot(xn, w_v[:, 3 * HD :]))
        kv_v[at, :HD] = jnp.where(live, keys, 0.0).astype(BF)
        values = silu(dot(xn, w_v[:, HD : 2 * HD]))
        kv_v[at, HD:] = jnp.where(live, values, 0.0).astype(BF)
        pltpu.make_async_copy(kv_v.at[at, :], kv_hbm.at[at, :], kv_sem).start()
        return carry

    send_group(2)
    send_group(3)
    lax.fori_loop(0, 6, encode_step, 0)
    first_span(msg, q_send).wait()
    remote_span(1, msg, q_send).wait()
    plane_rest = plane_in.at[pl.ds(8, 120), :]
    pltpu.make_async_copy(plane_rest, plane_rest, s_recv.at[1]).wait()

    half_scale = 0.5 * HDIM**-0.5

    def attend_group(grp):
        land_f[...] = land[pl.ds(grp * GSIZE, GSIZE)].astype(F32).reshape(GSIZE * MROWS, HDIM)
        lane = lax.broadcasted_iota(jnp.int32, (16, HDIM), 1)
        row = lax.broadcasted_iota(jnp.int32, (16, HDIM), 0)
        known = [plane_in[pl.ds(2 * grp + part, 16, stride=8), :] for part in range(2)]
        uid = jnp.concatenate(
            [
                jnp.broadcast_to(
                    jnp.sum(
                        jnp.where(lane == row + 16 * j, known[part], 0.0), axis=1, keepdims=True
                    ),
                    (16, HDIM),
                )
                for j in range(2 * CAP)
                for part in range(2)
            ],
            axis=0,
        )
        for h in range(HEADS):
            query = jnp.concatenate(
                [
                    land_f[pl.ds(cs * 12 + h * CAP + s, GSIZE, stride=MROWS), :]
                    for cs in range(2)
                    for s in range(CAP)
                ],
                axis=0,
            ).astype(BF)
            total = None
            for pair in range(USERS // 2):
                at = slice(pair * 256, pair * 256 + 256)
                score = dot_t(query, kv_v[at, h * HDIM : (h + 1) * HDIM]) * half_scale
                weight = score + score * jnp.tanh(score)
                mine = jnp.concatenate([uid == 2.0 * pair, uid == 2.0 * pair + 1.0], axis=1)
                weight = jnp.where(mine, weight, 0.0).astype(BF)
                part = dot(weight, kv_v[at, HD + h * HDIM : HD + (h + 1) * HDIM])
                total = part if total is None else total + part
            for j in range(2 * CAP):
                row_at = (j // CAP) * 12 + h * CAP + j % CAP
                ret_f[pl.ds(row_at, GSIZE, stride=MROWS), :] = total[
                    j * GSIZE : (j + 1) * GSIZE, :
                ]
        ret_msg[pl.ds(grp * GSIZE, GSIZE)] = ret_f[...].reshape(GSIZE, MROWS, HDIM).astype(BF)

    def send_back(j, carry):
        idx = (j // 32) * 32 + (j % 2) * 16 + (j % 32) // 2
        pltpu.make_async_remote_copy(
            src_ref=ret_msg.at[idx], dst_ref=ret_land.at[idx],
            send_sem=r_send.at[j // 32], recv_sem=r_recv.at[j // 32],
            device_id=peer(idx, -1), device_id_type=MESH,
        ).start()
        return carry

    first_span(land, q_recv).wait()
    attend_group(0)
    ret_land[0] = ret_msg[0]
    lax.fori_loop(1, GSIZE, send_back, 0)

    def group_step(grp, carry):
        remote_span(grp, land, q_recv).wait()
        attend_group(grp)
        lax.fori_loop(grp * GSIZE, grp * GSIZE + GSIZE, send_back, 0)
        return carry

    lax.fori_loop(1, GROUPS, group_step, 0)

    loads[4].wait()

    def own_step(i, carry):
        at = pl.ds(pl.multiple_of(i * 256, 256), 256)
        xn = xn_v[at, :]
        u_v[at, :] = silu(dot(xn, w_v[:, :HD])).astype(BF)
        own_v = silu(dot(xn, w_v[:, HD : 2 * HD])).astype(BF).astype(F32)
        own_k = silu(dot(xn, w_v[:, 3 * HD :])).astype(BF).astype(F32)
        prod = q_v[at, :].astype(F32) * own_k
        for h in range(HEADS):
            lanes = slice(h * HDIM, (h + 1) * HDIM)
            score = jnp.sum(prod[:, lanes], axis=-1, keepdims=True) * half_scale
            weight = (score + score * jnp.tanh(score)).astype(BF).astype(F32)
            att_v[at, lanes] = weight * own_v[:, lanes]
        return carry

    lax.fori_loop(0, 2, own_step, 0)
    place = (grp * 256 + (other * CAP + rank) * 32 + half * 16 + shift).astype(F32)
    place_col = jnp.sum(jnp.where(rows_i == cols_i, place, 0.0), axis=1, keepdims=True)
    lane_slot = lax.broadcasted_iota(jnp.int32, (CAND, GROUPS * 256), 1).astype(F32)
    place_v[...] = jnp.where(lane_slot == place_col, 1.0, 0.0).astype(BF)
    back_v[192:, :] = jnp.zeros((64, HD), BF)

    def hand_on(grp):
        span = pl.ds(grp * GSIZE, GSIZE)
        return pltpu.make_async_remote_copy(
            src_ref=ret_land.at[span], dst_ref=ret_sib.at[span],
            send_sem=f_send.at[grp], recv_sem=f_recv.at[grp],
            device_id=sibling, device_id_type=MESH,
        )

    def unpack(ref, grp, m):
        back_f[...] = ref[pl.ds(grp * GSIZE, GSIZE)].astype(F32).reshape(GSIZE * MROWS, HDIM)
        for s in range(CAP):
            first = (m * CAP + s) * GSIZE
            for h in range(HEADS):
                back_v[first : first + GSIZE, h * HDIM : (h + 1) * HDIM] = back_f[
                    pl.ds(c * 12 + h * CAP + s, GSIZE, stride=MROWS), :
                ].astype(BF)

    def take(grp):
        hand_on(grp).start()
        unpack(ret_land, grp, 0)
        hand_on(grp).wait()
        unpack(ret_sib, grp, 1)

    def gather(grp):
        def gather_step(i, carry):
            at = pl.ds(pl.multiple_of(i * 256, 256), 256)
            slots = pl.ds(pl.multiple_of(grp * 256, 256), 256)
            att_v[at, :] += dot(place_v[at, slots], back_v[...])
            return carry

        lax.fori_loop(0, 2, gather_step, 0)

    first_span(ret_land, r_recv).wait()
    take(0)
    gather(0)

    def take_step(grp, carry):
        remote_span(grp, ret_land, r_recv).wait()
        take(grp)
        gather(grp)
        return carry

    lax.fori_loop(1, GROUPS - 1, take_step, 0)
    remote_span(GROUPS - 1, ret_land, r_recv).wait()
    take(GROUPS - 1)

    def out_step(i, carry):
        at = pl.ds(pl.multiple_of(i * 256, 256), 256)
        last = dot(place_v[at, (GROUPS - 1) * 256 :], back_v[...])
        normed = norm_rows(att_v[at, :] + last).astype(BF).astype(F32)
        out_ref[at, :] = (normed * u_v[at, :].astype(F32)).astype(BF)
        return carry

    lax.fori_loop(0, 2, out_step, 0)

    remote_span(2, msg, q_send).wait()
    remote_span(3, msg, q_send).wait()
    first_span(ret_msg, r_send).wait()

    def sent(grp, carry):
        remote_span(grp, ret_msg, r_send).wait()
        return carry

    lax.fori_loop(1, GROUPS, sent, 0)
    pltpu.make_async_copy(ring_out.at[ring_rest], ring_out.at[ring_rest], s_send.at[0]).wait()
    pltpu.make_async_copy(plane_rest, plane_rest, s_send.at[1]).wait()
    pltpu.make_async_copy(kv_v, kv_hbm, kv_sem).wait()


def write_out(kv_ref, rows_ref, kv_out, rows_out, kv_v, rows_v, in_sem, out_sem):
    spans = [pl.ds(i * 192, 192) for i in range(8)]
    takes = [
        pltpu.make_async_copy(kv_ref.at[span, :], kv_v.at[span, :], in_sem.at[i])
        for i, span in enumerate(spans)
    ]
    puts = [
        pltpu.make_async_copy(kv_v.at[span, :], kv_out.at[span, :], out_sem.at[i])
        for i, span in enumerate(spans)
    ]
    takes.append(pltpu.make_async_copy(rows_ref, rows_v, in_sem.at[8]))
    puts.append(pltpu.make_async_copy(rows_v, rows_out, out_sem.at[8]))
    for take in takes:
        take.start()
    for take, put in zip(takes, puts):
        take.wait()
        put.start()
    for put in puts:
        put.wait()


def body(history, hist_len, cand, cand_owner, cand_user, norm_gain, w_proj):
    any_spec = pl.BlockSpec(memory_space=pl.ANY)
    vmem = pl.BlockSpec(memory_space=pltpu.VMEM)
    dma = pltpu.SemaphoreType.DMA
    results = (
        jax.ShapeDtypeStruct((USERS * ROWS, 2 * HD), BF),
        jax.ShapeDtypeStruct((CAND, HD), BF),
    )
    kv, out = pl.pallas_call(
        kernel,
        out_shape=results,
        in_specs=[
            pl.BlockSpec(memory_space=pltpu.SMEM), vmem, vmem, vmem, any_spec, any_spec, any_spec,
        ],
        out_specs=(any_spec, vmem),
        scratch_shapes=[
            pltpu.VMEM((CAND, D), BF),
            pltpu.VMEM((USERS * ROWS, D), BF),
            pltpu.VMEM((D, 4 * HD), BF),
            pltpu.VMEM((USERS * ROWS, 2 * HD), BF),
            pltpu.VMEM((CAND, D), BF),
            pltpu.VMEM((CAND, HD), BF),
            pltpu.VMEM((CAND, HD), BF),
            pltpu.VMEM((CAND, HD), F32),
            pltpu.VMEM((CAND, GROUPS * 256), BF),
            pltpu.VMEM((CAP, CHIPS, HD), BF),
            pltpu.VMEM((CAP, CHIPS, HD), BF),
            pltpu.VMEM((CHIPS * MROWS, HDIM), F32),
            pltpu.VMEM((CHIPS, MROWS, HDIM), BF),
            pltpu.VMEM((CHIPS, MROWS, HDIM), BF),
            pltpu.VMEM((GSIZE * MROWS, HDIM), F32),
            pltpu.VMEM((GSIZE * MROWS, HDIM), F32),
            pltpu.VMEM((CHIPS, MROWS, HDIM), BF),
            pltpu.VMEM((CHIPS, MROWS, HDIM), BF),
            pltpu.VMEM((CHIPS, MROWS, HDIM), BF),
            pltpu.VMEM((GSIZE * MROWS, HDIM), F32),
            pltpu.VMEM((256, HD), BF),
            pltpu.VMEM((8, HDIM), F32),
            pltpu.VMEM((8, HDIM), F32),
            pltpu.VMEM((8, 1, HDIM), F32),
            pltpu.VMEM((8, 1, HDIM), F32),
            pltpu.VMEM((8, HDIM), F32),
            pltpu.VMEM((HDIM, HDIM), F32),
            dma((6,)),
            dma,
            dma((CAP + 1,)),
            dma((CAP + 1,)),
            pltpu.SemaphoreType.REGULAR,
            dma((GROUPS,)),
            dma((GROUPS,)),
            dma((GROUPS,)),
            dma((GROUPS,)),
            dma((GROUPS,)),
            dma((GROUPS,)),
            dma((2,)),
            dma((2,)),
        ],
        compiler_params=pltpu.CompilerParams(
            collective_id=0, has_side_effects=True, vmem_limit_bytes=56 << 20
        ),
        cost_estimate=pl.CostEstimate(
            flops=12_000_000_000, bytes_accessed=12_000_000, transcendentals=8_000_000
        ),
        name="routed_attention",
    )(
        hist_len,
        cand_owner.reshape(1, CAND),
        cand_user.reshape(1, CAND),
        norm_gain.reshape(1, D),
        cand,
        history.reshape(USERS * ROWS, D),
        w_proj,
    )
    kv, out = pl.pallas_call(
        write_out,
        out_shape=results,
        in_specs=[any_spec, any_spec],
        out_specs=(any_spec, any_spec),
        scratch_shapes=[
            pltpu.VMEM((USERS * ROWS, 2 * HD), BF), pltpu.VMEM((CAND, HD), BF), dma((9,)), dma((9,)),
        ],
        name="write_out",
    )(kv, out)
    return kv.reshape(USERS, ROWS, 2 * HD), out


def solution(mesh):
    placed = (
        P(("grp", "enc"), None, None),
        P(("grp", "enc")),
        P(("grp", "enc"), None),
        P(("grp", "enc"), None),
        P(("grp", "enc")),
        P(),
        P(),
    )
    return jax.shard_map(
        body,
        mesh=mesh,
        in_specs=placed,
        out_specs=(P(("grp", "enc"), None, None), P(("grp", "enc"), None)),
        check_vma=False,
    )
```

```python
import functools

import jax
import jax.numpy as jnp
from jax import lax
from jax.experimental import pallas as pl
from jax.experimental.pallas import tpu as pltpu
from jax.sharding import PartitionSpec as P

MESH = pl.DeviceIdType.MESH
HDIM = 128
HEADS = 4
HD = 512
D = 1024
PIECE = 64
ROWS = 128
USERS = 12
CAND = 512
CAP = 3
CHIPS = 128
GROUPS = 4
GSIZE = 32
MROWS = 24
BF = jnp.bfloat16
F32 = jnp.float32


def silu(x):
    half = 0.5 * x
    return half + half * jnp.tanh(half)


def norm_rows(x):
    center = x - jnp.mean(x, axis=-1, keepdims=True)
    spread = jnp.mean(center * center, axis=-1, keepdims=True)
    return center * lax.rsqrt(spread + 1e-5)


def dot(a, b):
    return jnp.dot(a, b, preferred_element_type=F32)


def dot_t(a, b):
    return lax.dot_general(a, b, (((1,), (1,)), ((), ())), preferred_element_type=F32)


def kernel(
    len_ref, owner_ref, user_ref, gain_ref, cand_hbm, hist_hbm, w_hbm,
    kv_v, out_ref,
    cand_v, hist_v, w_v, xn_v, q_v, u_v, att_v, place_v,
    sib_out, sib_in, tab, msg, land, land_f, ret_f, ret_msg, ret_land, ret_sib, back_f, back_v,
    slot_out, slot_in, ring_out, ring_in, plane_out, plane_in,
    load_sem, sib_send, sib_recv, ready_sem,
    q_send, q_recv, r_send, r_recv, f_send, f_recv, s_send, s_recv,
):
    g, e = lax.axis_index("grp"), lax.axis_index("enc")
    y, x, c = e // 8, (e // 2) % 4, e % 2
    sibling = (g, y * 8 + x * 2 + 1 - c)

    def plane_peer(k):
        return g, ((y + k // 4) % 4) * 8 + ((x + k % 4) % 4) * 2 + c

    def ring_shift(r):
        return (1 - r % 2) * ((4 - r // 2) % 4) + (r % 2) * (4 + r // 2)

    def peer(idx, sign):
        dz, k = ring_shift(idx // 16), idx % 16
        py = (y + sign * (k // 4) + 4) % 4
        px = (x + sign * (k % 4) + 4) % 4
        return (g + sign * dz + 8) % 8, py * 8 + px * 2 + c

    cols = [(2 * HD, 3 * HD), (3 * HD, 4 * HD), (HD, 2 * HD), (0, HD)]
    loads = [pltpu.make_async_copy(cand_hbm, cand_v, load_sem.at[0])]
    for i, (lo, hi) in enumerate(cols):
        loads.append(
            pltpu.make_async_copy(
                w_hbm.at[:, pl.ds(lo, HD)], w_v.at[:, pl.ds(lo, HD)], load_sem.at[1 + i]
            )
        )
    loads.append(pltpu.make_async_copy(hist_hbm, hist_v, load_sem.at[5]))
    for i in (0, 1, 5, 2, 3, 4):
        loads[i].start()

    barrier = pltpu.get_barrier_semaphore()

    def greet_ring(k, carry):
        pl.semaphore_signal(
            barrier, inc=1, device_id=((g + k) % 8, e), device_id_type=MESH
        )
        return carry

    def greet_plane(k, carry):
        pl.semaphore_signal(barrier, inc=1, device_id=plane_peer(k), device_id_type=MESH)
        return carry

    lax.fori_loop(1, 8, greet_ring, 0)
    lax.fori_loop(1, 16, greet_plane, 0)
    pl.semaphore_signal(barrier, inc=1, device_id=sibling, device_id_type=MESH)

    rows_i = lax.broadcasted_iota(jnp.int32, (CAND, CAND), 0)
    cols_i = lax.broadcasted_iota(jnp.int32, (CAND, CAND), 1)
    owner = owner_ref[...]
    owner_f = owner.astype(F32)
    owner_col = jnp.sum(jnp.where(rows_i == cols_i, owner_f, 0.0), axis=1, keepdims=True)
    same = (owner_col == owner_f) & (rows_i < cols_i)
    rank = jnp.sum(jnp.where(same, 1.0, 0.0), axis=0, keepdims=True).astype(jnp.int32)
    to_g, to_e = owner // 32, owner % 32
    dz = (to_g - g + 8) % 8
    half = dz // 4
    grp = jnp.where(half == 1, dz - 4, (4 - dz) % 4)
    ry = (to_e // 8 - y + 4) % 4
    rx = ((to_e // 2) % 4 - x + 4) % 4
    other = jnp.where(to_e % 2 == c, 0, 1)
    shift = ry * 4 + rx
    code = (other * CAP + rank) * CHIPS + grp * 32 + half * 16 + shift

    def pick(j):
        slot = lax.broadcasted_iota(jnp.int32, (CHIPS, CAND), 0) + j * CHIPS
        return jnp.where(slot == code, 1.0, 0.0).astype(BF)

    ring_row = lax.broadcasted_iota(jnp.int32, (8, CAND), 0) + 8 * other
    slot_lane = lax.broadcasted_iota(jnp.int32, (HDIM, CAND), 0)
    lane_hot = jnp.where(slot_lane == (c * CAP + rank) * 16 + shift, 1.0, 0.0).astype(BF)
    user_f = user_ref[...].astype(F32)

    def slot_users(m):
        mine = ring_row == grp * 2 + half + 8 * m
        return dot_t(jnp.where(mine, user_f, 0.0).astype(BF), lane_hot)

    slot_out[...] = slot_users(1)

    gain = gain_ref[...]
    loads[0].wait()
    loads[1].wait()

    def query_step(i, carry):
        at = pl.ds(pl.multiple_of(i * 256, 256), 256)
        xn = (norm_rows(cand_v[at, :].astype(F32)) * gain).astype(BF)
        xn_v[at, :] = xn
        q_v[at, :] = silu(dot(xn, w_v[:, 2 * HD : 3 * HD])).astype(BF)
        return carry

    lax.fori_loop(0, 2, query_step, 0)

    def swap(s):
        return pltpu.make_async_remote_copy(
            src_ref=sib_out.at[s], dst_ref=sib_in.at[s],
            send_sem=sib_send.at[s], recv_sem=sib_recv.at[s],
            device_id=sibling, device_id_type=MESH,
        )

    swap_users = pltpu.make_async_remote_copy(
        src_ref=slot_out, dst_ref=slot_in, send_sem=sib_send.at[CAP], recv_sem=sib_recv.at[CAP],
        device_id=sibling, device_id_type=MESH,
    )

    for s in range(CAP):
        sib_out[s] = dot(pick(CAP + s), q_v[...]).astype(BF)
        if s == 0:
            pl.semaphore_wait(barrier, 23)
            swap_users.start()
        swap(s).start()

    def say_ready(k, carry):
        pl.semaphore_signal(ready_sem, inc=1, device_id=plane_peer(k), device_id_type=MESH)
        return carry

    lax.fori_loop(1, 16, say_ready, 0)

    def lay(rows, core, s):
        for h in range(HEADS):
            tab[pl.ds(core * 12 + h * CAP + s, CHIPS, stride=MROWS), :] = rows[
                :, h * HDIM : (h + 1) * HDIM
            ]

    for s in range(CAP):
        lay(dot(pick(s), q_v[...]), c, s)
    own_users = slot_users(0)
    swap_users.wait()
    ring_out[...] = (own_users + slot_in[...]).reshape(8, 1, HDIM)
    ring_in[0] = ring_out[0]

    def send_ring(r, carry):
        pltpu.make_async_remote_copy(
            src_ref=ring_out.at[r], dst_ref=ring_in.at[r],
            send_sem=s_send.at[0], recv_sem=s_recv.at[0],
            device_id=((g + ring_shift(r)) % 8, e), device_id_type=MESH,
        ).start()
        return carry

    lax.fori_loop(1, 8, send_ring, 0)

    for s in range(CAP):
        swap(s).wait()
        lay(sib_in[s].astype(F32), 1 - c, s)
    pl.semaphore_wait(ready_sem, 15)

    def send_query(j, carry):
        idx = (j // 32) * 32 + (j % 2) * 16 + (j % 32) // 2
        pltpu.make_async_remote_copy(
            src_ref=msg.at[idx], dst_ref=land.at[idx],
            send_sem=q_send.at[j // 32], recv_sem=q_recv.at[j // 32],
            device_id=peer(idx, 1), device_id_type=MESH,
        ).start()
        return carry

    def fill(grp):
        rows = pl.ds(grp * GSIZE * MROWS, GSIZE * MROWS)
        msg[pl.ds(grp * GSIZE, GSIZE)] = tab[rows, :].reshape(GSIZE, MROWS, HDIM).astype(BF)

    def send_group(grp):
        lax.fori_loop(grp * GSIZE, grp * GSIZE + GSIZE, send_query, 0)

    fill(0)
    lax.fori_loop(1, GSIZE, send_query, 0)
    fill(1)

    ring_rest = pl.ds(1, 7)
    pltpu.make_async_copy(ring_in.at[ring_rest], ring_in.at[ring_rest], s_recv.at[0]).wait()
    plane_out[...] = ring_in[...].reshape(8, HDIM)
    plane_in[0:8, :] = plane_out[...]

    def send_plane(k, carry):
        pltpu.make_async_remote_copy(
            src_ref=plane_out, dst_ref=plane_in.at[pl.ds(k * 8, 8), :],
            send_sem=s_send.at[1], recv_sem=s_recv.at[1],
            device_id=plane_peer(k), device_id_type=MESH,
        ).start()
        return carry

    lax.fori_loop(1, 16, send_plane, 0)

    send_group(1)
    land[0] = msg[0]
    fill(2)
    fill(3)

    def remote_span(grp, ref, sem):
        return pltpu.make_async_copy(
            ref.at[pl.ds(grp * GSIZE, GSIZE)], ref.at[pl.ds(grp * GSIZE, GSIZE)], sem.at[grp]
        )

    def first_span(ref, sem):
        return pltpu.make_async_copy(
            ref.at[pl.ds(1, GSIZE - 1)], ref.at[pl.ds(1, GSIZE - 1)], sem.at[0]
        )

    loads[2].wait()
    loads[3].wait()
    loads[5].wait()

    def encode_step(i, carry):
        at = pl.ds(pl.multiple_of(i * 256, 256), 256)
        xn = (norm_rows(hist_v[at, :].astype(F32)) * gain).astype(BF)
        row = lax.broadcasted_iota(jnp.int32, (256, HD), 0)
        live = row < jnp.where(
            row < ROWS, len_ref[2 * i] * PIECE, len_ref[2 * i + 1] * PIECE + ROWS
        )
        keys = silu(dot(xn, w_v[:, 3 * HD :]))
        kv_v[at, :HD] = jnp.where(live, keys, 0.0).astype(BF)
        values = silu(dot(xn, w_v[:, HD : 2 * HD]))
        kv_v[at, HD:] = jnp.where(live, values, 0.0).astype(BF)
        return carry

    send_group(2)
    send_group(3)
    lax.fori_loop(0, 6, encode_step, 0)
    first_span(msg, q_send).wait()
    remote_span(1, msg, q_send).wait()
    plane_rest = plane_in.at[pl.ds(8, 120), :]
    pltpu.make_async_copy(plane_rest, plane_rest, s_recv.at[1]).wait()

    half_scale = 0.5 * HDIM**-0.5

    def attend_group(grp):
        land_f[...] = land[pl.ds(grp * GSIZE, GSIZE)].astype(F32).reshape(GSIZE * MROWS, HDIM)
        lane = lax.broadcasted_iota(jnp.int32, (16, HDIM), 1)
        row = lax.broadcasted_iota(jnp.int32, (16, HDIM), 0)
        known = [plane_in[pl.ds(2 * grp + part, 16, stride=8), :] for part in range(2)]
        uid = jnp.concatenate(
            [
                jnp.broadcast_to(
                    jnp.sum(
                        jnp.where(lane == row + 16 * j, known[part], 0.0), axis=1, keepdims=True
                    ),
                    (16, HDIM),
                )
                for j in range(2 * CAP)
                for part in range(2)
            ],
            axis=0,
        )
        for h in range(HEADS):
            query = jnp.concatenate(
                [
                    land_f[pl.ds(cs * 12 + h * CAP + s, GSIZE, stride=MROWS), :]
                    for cs in range(2)
                    for s in range(CAP)
                ],
                axis=0,
            ).astype(BF)
            total = None
            for pair in range(USERS // 2):
                at = slice(pair * 256, pair * 256 + 256)
                score = dot_t(query, kv_v[at, h * HDIM : (h + 1) * HDIM]) * half_scale
                weight = score + score * jnp.tanh(score)
                mine = jnp.concatenate([uid == 2.0 * pair, uid == 2.0 * pair + 1.0], axis=1)
                weight = jnp.where(mine, weight, 0.0).astype(BF)
                part = dot(weight, kv_v[at, HD + h * HDIM : HD + (h + 1) * HDIM])
                total = part if total is None else total + part
            for j in range(2 * CAP):
                row_at = (j // CAP) * 12 + h * CAP + j % CAP
                ret_f[pl.ds(row_at, GSIZE, stride=MROWS), :] = total[
                    j * GSIZE : (j + 1) * GSIZE, :
                ]
        ret_msg[pl.ds(grp * GSIZE, GSIZE)] = ret_f[...].reshape(GSIZE, MROWS, HDIM).astype(BF)

    def send_back(j, carry):
        idx = (j // 32) * 32 + (j % 2) * 16 + (j % 32) // 2
        pltpu.make_async_remote_copy(
            src_ref=ret_msg.at[idx], dst_ref=ret_land.at[idx],
            send_sem=r_send.at[j // 32], recv_sem=r_recv.at[j // 32],
            device_id=peer(idx, -1), device_id_type=MESH,
        ).start()
        return carry

    first_span(land, q_recv).wait()
    attend_group(0)
    ret_land[0] = ret_msg[0]
    lax.fori_loop(1, GSIZE, send_back, 0)

    def group_step(grp, carry):
        remote_span(grp, land, q_recv).wait()
        attend_group(grp)
        lax.fori_loop(grp * GSIZE, grp * GSIZE + GSIZE, send_back, 0)
        return carry

    lax.fori_loop(1, GROUPS, group_step, 0)

    loads[4].wait()

    def own_step(i, carry):
        at = pl.ds(pl.multiple_of(i * 256, 256), 256)
        xn = xn_v[at, :]
        u_v[at, :] = silu(dot(xn, w_v[:, :HD])).astype(BF)
        own_v = silu(dot(xn, w_v[:, HD : 2 * HD])).astype(BF).astype(F32)
        own_k = silu(dot(xn, w_v[:, 3 * HD :])).astype(BF).astype(F32)
        prod = q_v[at, :].astype(F32) * own_k
        for h in range(HEADS):
            lanes = slice(h * HDIM, (h + 1) * HDIM)
            score = jnp.sum(prod[:, lanes], axis=-1, keepdims=True) * half_scale
            weight = (score + score * jnp.tanh(score)).astype(BF).astype(F32)
            att_v[at, lanes] = weight * own_v[:, lanes]
        return carry

    lax.fori_loop(0, 2, own_step, 0)
    place = (grp * 256 + (other * CAP + rank) * 32 + half * 16 + shift).astype(F32)
    place_col = jnp.sum(jnp.where(rows_i == cols_i, place, 0.0), axis=1, keepdims=True)
    lane_slot = lax.broadcasted_iota(jnp.int32, (CAND, GROUPS * 256), 1).astype(F32)
    place_v[...] = jnp.where(lane_slot == place_col, 1.0, 0.0).astype(BF)
    back_v[192:, :] = jnp.zeros((64, HD), BF)

    def hand_on(grp):
        span = pl.ds(grp * GSIZE, GSIZE)
        return pltpu.make_async_remote_copy(
            src_ref=ret_land.at[span], dst_ref=ret_sib.at[span],
            send_sem=f_send.at[grp], recv_sem=f_recv.at[grp],
            device_id=sibling, device_id_type=MESH,
        )

    def unpack(ref, grp, m):
        back_f[...] = ref[pl.ds(grp * GSIZE, GSIZE)].astype(F32).reshape(GSIZE * MROWS, HDIM)
        for s in range(CAP):
            first = (m * CAP + s) * GSIZE
            for h in range(HEADS):
                back_v[first : first + GSIZE, h * HDIM : (h + 1) * HDIM] = back_f[
                    pl.ds(c * 12 + h * CAP + s, GSIZE, stride=MROWS), :
                ].astype(BF)

    def take(grp):
        hand_on(grp).start()
        unpack(ret_land, grp, 0)
        hand_on(grp).wait()
        unpack(ret_sib, grp, 1)

    def gather(grp):
        def gather_step(i, carry):
            at = pl.ds(pl.multiple_of(i * 256, 256), 256)
            slots = pl.ds(pl.multiple_of(grp * 256, 256), 256)
            att_v[at, :] += dot(place_v[at, slots], back_v[...])
            return carry

        lax.fori_loop(0, 2, gather_step, 0)

    first_span(ret_land, r_recv).wait()
    take(0)
    gather(0)

    def take_step(grp, carry):
        remote_span(grp, ret_land, r_recv).wait()
        take(grp)
        gather(grp)
        return carry

    lax.fori_loop(1, GROUPS - 1, take_step, 0)
    remote_span(GROUPS - 1, ret_land, r_recv).wait()
    take(GROUPS - 1)

    def out_step(i, carry):
        at = pl.ds(pl.multiple_of(i * 256, 256), 256)
        last = dot(place_v[at, (GROUPS - 1) * 256 :], back_v[...])
        normed = norm_rows(att_v[at, :] + last).astype(BF).astype(F32)
        out_ref[at, :] = (normed * u_v[at, :].astype(F32)).astype(BF)
        return carry

    lax.fori_loop(0, 2, out_step, 0)

    remote_span(2, msg, q_send).wait()
    remote_span(3, msg, q_send).wait()
    first_span(ret_msg, r_send).wait()

    def sent(grp, carry):
        remote_span(grp, ret_msg, r_send).wait()
        return carry

    lax.fori_loop(1, GROUPS, sent, 0)
    pltpu.make_async_copy(ring_out.at[ring_rest], ring_out.at[ring_rest], s_send.at[0]).wait()
    pltpu.make_async_copy(plane_rest, plane_rest, s_send.at[1]).wait()


def body(history, hist_len, cand, cand_owner, cand_user, norm_gain, w_proj):
    any_spec = pl.BlockSpec(memory_space=pl.ANY)
    vmem = pl.BlockSpec(memory_space=pltpu.VMEM)
    dma = pltpu.SemaphoreType.DMA
    kv, out = pl.pallas_call(
        kernel,
        out_shape=(
            pltpu.VMEM((USERS * ROWS, 2 * HD), BF), pltpu.VMEM((CAND, HD), BF),
        ),
        in_specs=[
            pl.BlockSpec(memory_space=pltpu.SMEM), vmem, vmem, vmem, any_spec, any_spec, any_spec,
        ],
        out_specs=(vmem, vmem),
        scratch_shapes=[
            pltpu.VMEM((CAND, D), BF),
            pltpu.VMEM((USERS * ROWS, D), BF),
            pltpu.VMEM((D, 4 * HD), BF),
            pltpu.VMEM((CAND, D), BF),
            pltpu.VMEM((CAND, HD), BF),
            pltpu.VMEM((CAND, HD), BF),
            pltpu.VMEM((CAND, HD), F32),
            pltpu.VMEM((CAND, GROUPS * 256), BF),
            pltpu.VMEM((CAP, CHIPS, HD), BF),
            pltpu.VMEM((CAP, CHIPS, HD), BF),
            pltpu.VMEM((CHIPS * MROWS, HDIM), F32),
            pltpu.VMEM((CHIPS, MROWS, HDIM), BF),
            pltpu.VMEM((CHIPS, MROWS, HDIM), BF),
            pltpu.VMEM((GSIZE * MROWS, HDIM), F32),
            pltpu.VMEM((GSIZE * MROWS, HDIM), F32),
            pltpu.VMEM((CHIPS, MROWS, HDIM), BF),
            pltpu.VMEM((CHIPS, MROWS, HDIM), BF),
            pltpu.VMEM((CHIPS, MROWS, HDIM), BF),
            pltpu.VMEM((GSIZE * MROWS, HDIM), F32),
            pltpu.VMEM((256, HD), BF),
            pltpu.VMEM((8, HDIM), F32),
            pltpu.VMEM((8, HDIM), F32),
            pltpu.VMEM((8, 1, HDIM), F32),
            pltpu.VMEM((8, 1, HDIM), F32),
            pltpu.VMEM((8, HDIM), F32),
            pltpu.VMEM((HDIM, HDIM), F32),
            dma((6,)),
            dma((CAP + 1,)),
            dma((CAP + 1,)),
            pltpu.SemaphoreType.REGULAR,
            dma((GROUPS,)),
            dma((GROUPS,)),
            dma((GROUPS,)),
            dma((GROUPS,)),
            dma((GROUPS,)),
            dma((GROUPS,)),
            dma((2,)),
            dma((2,)),
        ],
        compiler_params=pltpu.CompilerParams(
            collective_id=0, has_side_effects=True, vmem_limit_bytes=58 << 20
        ),
        cost_estimate=pl.CostEstimate(
            flops=12_000_000_000, bytes_accessed=12_000_000, transcendentals=8_000_000
        ),
        name="routed_attention",
    )(
        hist_len,
        cand_owner.reshape(1, CAND),
        cand_user.reshape(1, CAND),
        norm_gain.reshape(1, D),
        cand,
        history.reshape(USERS * ROWS, D),
        w_proj,
    )
    return kv.reshape(USERS, ROWS, 2 * HD), out


def solution(mesh):
    placed = (
        P(("grp", "enc"), None, None),
        P(("grp", "enc")),
        P(("grp", "enc"), None),
        P(("grp", "enc"), None),
        P(("grp", "enc")),
        P(),
        P(),
    )
    return jax.shard_map(
        body,
        mesh=mesh,
        in_specs=placed,
        out_specs=(P(("grp", "enc"), None, None), P(("grp", "enc"), None)),
        check_vma=False,
    )
```

```python
import functools

import jax
import jax.numpy as jnp
from jax import lax
from jax.experimental import pallas as pl
from jax.experimental.pallas import tpu as pltpu
from jax.sharding import PartitionSpec as P

MESH = pl.DeviceIdType.MESH
HDIM = 128
HEADS = 4
HD = 512
D = 1024
PIECE = 64
ROWS = 128
USERS = 12
CAND = 512
CAP = 3
CHIPS = 128
GROUPS = 4
GSIZE = 32
MROWS = 24
BF = jnp.bfloat16
F32 = jnp.float32


def silu(x):
    half = 0.5 * x
    return half + half * jnp.tanh(half)


def norm_rows(x):
    center = x - jnp.mean(x, axis=-1, keepdims=True)
    spread = jnp.mean(center * center, axis=-1, keepdims=True)
    return center * lax.rsqrt(spread + 1e-5)


def dot(a, b):
    return jnp.dot(a, b, preferred_element_type=F32)


def dot_t(a, b):
    return lax.dot_general(a, b, (((1,), (1,)), ((), ())), preferred_element_type=F32)


def kernel(
    len_ref, owner_ref, user_ref, gain_ref, cand_hbm, hist_hbm, w_hbm,
    kv_v, out_ref,
    cand_v, hist_v, w_v, xn_v, q_v, u_v, att_v, place_v,
    sib_out, sib_in, tab, msg, land, land_f, ret_f, ret_msg, ret_land, ret_sib, back_f, back_v,
    slot_out, slot_in, ring_out, ring_in, plane_out, plane_in,
    load_sem, sib_send, sib_recv, ready_sem,
    q_send, q_recv, r_send, r_recv, f_send, f_recv, s_send, s_recv,
):
    g, e = lax.axis_index("grp"), lax.axis_index("enc")
    y, x, c = e // 8, (e // 2) % 4, e % 2
    sibling = (g, y * 8 + x * 2 + 1 - c)

    def plane_peer(k):
        return g, ((y + k // 4) % 4) * 8 + ((x + k % 4) % 4) * 2 + c

    def ring_shift(r):
        return (1 - r % 2) * ((4 - r // 2) % 4) + (r % 2) * (4 + r // 2)

    def peer(idx, sign):
        dz, k = ring_shift(idx // 16), idx % 16
        py = (y + sign * (k // 4) + 4) % 4
        px = (x + sign * (k % 4) + 4) % 4
        return (g + sign * dz + 8) % 8, py * 8 + px * 2 + c

    cols = [(2 * HD, 3 * HD), (3 * HD, 4 * HD), (HD, 2 * HD), (0, HD)]
    loads = [pltpu.make_async_copy(cand_hbm, cand_v, load_sem.at[0])]
    for i, (lo, hi) in enumerate(cols):
        loads.append(
            pltpu.make_async_copy(
                w_hbm.at[:, pl.ds(lo, HD)], w_v.at[:, pl.ds(lo, HD)], load_sem.at[1 + i]
            )
        )
    loads.append(pltpu.make_async_copy(hist_hbm, hist_v, load_sem.at[5]))
    for i in (0, 1):
        loads[i].start()

    barrier = pltpu.get_barrier_semaphore()

    def greet_ring(k, carry):
        pl.semaphore_signal(
            barrier, inc=1, device_id=((g + k) % 8, e), device_id_type=MESH
        )
        return carry

    def greet_plane(k, carry):
        pl.semaphore_signal(barrier, inc=1, device_id=plane_peer(k), device_id_type=MESH)
        return carry

    lax.fori_loop(1, 8, greet_ring, 0)
    lax.fori_loop(1, 16, greet_plane, 0)
    pl.semaphore_signal(barrier, inc=1, device_id=sibling, device_id_type=MESH)

    rows_i = lax.broadcasted_iota(jnp.int32, (CAND, CAND), 0)
    cols_i = lax.broadcasted_iota(jnp.int32, (CAND, CAND), 1)
    owner = owner_ref[...]
    owner_f = owner.astype(F32)
    owner_col = jnp.sum(jnp.where(rows_i == cols_i, owner_f, 0.0), axis=1, keepdims=True)
    same = (owner_col == owner_f) & (rows_i < cols_i)
    rank = jnp.sum(jnp.where(same, 1.0, 0.0), axis=0, keepdims=True).astype(jnp.int32)
    to_g, to_e = owner // 32, owner % 32
    dz = (to_g - g + 8) % 8
    half = dz // 4
    grp = jnp.where(half == 1, dz - 4, (4 - dz) % 4)
    ry = (to_e // 8 - y + 4) % 4
    rx = ((to_e // 2) % 4 - x + 4) % 4
    other = jnp.where(to_e % 2 == c, 0, 1)
    shift = ry * 4 + rx
    code = (other * CAP + rank) * CHIPS + grp * 32 + half * 16 + shift

    def pick(j):
        slot = lax.broadcasted_iota(jnp.int32, (CHIPS, CAND), 0) + j * CHIPS
        return jnp.where(slot == code, 1.0, 0.0).astype(BF)

    ring_row = lax.broadcasted_iota(jnp.int32, (8, CAND), 0) + 8 * other
    slot_lane = lax.broadcasted_iota(jnp.int32, (HDIM, CAND), 0)
    lane_hot = jnp.where(slot_lane == (c * CAP + rank) * 16 + shift, 1.0, 0.0).astype(BF)
    user_f = user_ref[...].astype(F32)

    def slot_users(m):
        mine = ring_row == grp * 2 + half + 8 * m
        return dot_t(jnp.where(mine, user_f, 0.0).astype(BF), lane_hot)

    slot_out[...] = slot_users(1)

    gain = gain_ref[...]
    loads[0].wait()
    loads[1].wait()
    for i in (5, 2, 3, 4):
        loads[i].start()

    def query_step(i, carry):
        at = pl.ds(pl.multiple_of(i * 256, 256), 256)
        xn = (norm_rows(cand_v[at, :].astype(F32)) * gain).astype(BF)
        xn_v[at, :] = xn
        q_v[at, :] = silu(dot(xn, w_v[:, 2 * HD : 3 * HD])).astype(BF)
        return carry

    lax.fori_loop(0, 2, query_step, 0)

    def swap(s):
        return pltpu.make_async_remote_copy(
            src_ref=sib_out.at[s], dst_ref=sib_in.at[s],
            send_sem=sib_send.at[s], recv_sem=sib_recv.at[s],
            device_id=sibling, device_id_type=MESH,
        )

    swap_users = pltpu.make_async_remote_copy(
        src_ref=slot_out, dst_ref=slot_in, send_sem=sib_send.at[CAP], recv_sem=sib_recv.at[CAP],
        device_id=sibling, device_id_type=MESH,
    )

    for s in range(CAP):
        sib_out[s] = dot(pick(CAP + s), q_v[...]).astype(BF)
        if s == 0:
            pl.semaphore_wait(barrier, 23)
            swap_users.start()
        swap(s).start()

    def say_ready(k, carry):
        pl.semaphore_signal(ready_sem, inc=1, device_id=plane_peer(k), device_id_type=MESH)
        return carry

    lax.fori_loop(1, 16, say_ready, 0)

    def lay(rows, core, s):
        for h in range(HEADS):
            tab[pl.ds(core * 12 + h * CAP + s, CHIPS, stride=MROWS), :] = rows[
                :, h * HDIM : (h + 1) * HDIM
            ]

    for s in range(CAP):
        lay(dot(pick(s), q_v[...]), c, s)
    own_users = slot_users(0)
    swap_users.wait()
    ring_out[...] = (own_users + slot_in[...]).reshape(8, 1, HDIM)
    ring_in[0] = ring_out[0]

    def send_ring(r, carry):
        pltpu.make_async_remote_copy(
            src_ref=ring_out.at[r], dst_ref=ring_in.at[r],
            send_sem=s_send.at[0], recv_sem=s_recv.at[0],
            device_id=((g + ring_shift(r)) % 8, e), device_id_type=MESH,
        ).start()
        return carry

    lax.fori_loop(1, 8, send_ring, 0)

    for s in range(CAP):
        swap(s).wait()
        lay(sib_in[s].astype(F32), 1 - c, s)
    pl.semaphore_wait(ready_sem, 15)

    def send_query(j, carry):
        idx = (j // 32) * 32 + (j % 2) * 16 + (j % 32) // 2
        pltpu.make_async_remote_copy(
            src_ref=msg.at[idx], dst_ref=land.at[idx],
            send_sem=q_send.at[j // 32], recv_sem=q_recv.at[j // 32],
            device_id=peer(idx, 1), device_id_type=MESH,
        ).start()
        return carry

    def fill(grp):
        rows = pl.ds(grp * GSIZE * MROWS, GSIZE * MROWS)
        msg[pl.ds(grp * GSIZE, GSIZE)] = tab[rows, :].reshape(GSIZE, MROWS, HDIM).astype(BF)

    def send_group(grp):
        lax.fori_loop(grp * GSIZE, grp * GSIZE + GSIZE, send_query, 0)

    fill(0)
    lax.fori_loop(1, GSIZE, send_query, 0)
    fill(1)

    ring_rest = pl.ds(1, 7)
    pltpu.make_async_copy(ring_in.at[ring_rest], ring_in.at[ring_rest], s_recv.at[0]).wait()
    plane_out[...] = ring_in[...].reshape(8, HDIM)
    plane_in[0:8, :] = plane_out[...]

    def send_plane(k, carry):
        pltpu.make_async_remote_copy(
            src_ref=plane_out, dst_ref=plane_in.at[pl.ds(k * 8, 8), :],
            send_sem=s_send.at[1], recv_sem=s_recv.at[1],
            device_id=plane_peer(k), device_id_type=MESH,
        ).start()
        return carry

    lax.fori_loop(1, 16, send_plane, 0)

    send_group(1)
    land[0] = msg[0]
    fill(2)
    fill(3)

    def remote_span(grp, ref, sem):
        return pltpu.make_async_copy(
            ref.at[pl.ds(grp * GSIZE, GSIZE)], ref.at[pl.ds(grp * GSIZE, GSIZE)], sem.at[grp]
        )

    def first_span(ref, sem):
        return pltpu.make_async_copy(
            ref.at[pl.ds(1, GSIZE - 1)], ref.at[pl.ds(1, GSIZE - 1)], sem.at[0]
        )

    loads[2].wait()
    loads[3].wait()
    loads[5].wait()

    def encode_step(i, carry):
        at = pl.ds(pl.multiple_of(i * 256, 256), 256)
        xn = (norm_rows(hist_v[at, :].astype(F32)) * gain).astype(BF)
        row = lax.broadcasted_iota(jnp.int32, (256, HD), 0)
        live = row < jnp.where(
            row < ROWS, len_ref[2 * i] * PIECE, len_ref[2 * i + 1] * PIECE + ROWS
        )
        keys = silu(dot(xn, w_v[:, 3 * HD :]))
        kv_v[at, :HD] = jnp.where(live, keys, 0.0).astype(BF)
        values = silu(dot(xn, w_v[:, HD : 2 * HD]))
        kv_v[at, HD:] = jnp.where(live, values, 0.0).astype(BF)
        return carry

    send_group(2)
    send_group(3)
    lax.fori_loop(0, 6, encode_step, 0)
    first_span(msg, q_send).wait()
    remote_span(1, msg, q_send).wait()
    plane_rest = plane_in.at[pl.ds(8, 120), :]
    pltpu.make_async_copy(plane_rest, plane_rest, s_recv.at[1]).wait()

    half_scale = 0.5 * HDIM**-0.5

    def attend_group(grp):
        land_f[...] = land[pl.ds(grp * GSIZE, GSIZE)].astype(F32).reshape(GSIZE * MROWS, HDIM)
        lane = lax.broadcasted_iota(jnp.int32, (16, HDIM), 1)
        row = lax.broadcasted_iota(jnp.int32, (16, HDIM), 0)
        known = [plane_in[pl.ds(2 * grp + part, 16, stride=8), :] for part in range(2)]
        uid = jnp.concatenate(
            [
                jnp.broadcast_to(
                    jnp.sum(
                        jnp.where(lane == row + 16 * j, known[part], 0.0), axis=1, keepdims=True
                    ),
                    (16, HDIM),
                )
                for j in range(2 * CAP)
                for part in range(2)
            ],
            axis=0,
        )
        for h in range(HEADS):
            query = jnp.concatenate(
                [
                    land_f[pl.ds(cs * 12 + h * CAP + s, GSIZE, stride=MROWS), :]
                    for cs in range(2)
                    for s in range(CAP)
                ],
                axis=0,
            ).astype(BF)
            total = None
            for pair in range(USERS // 2):
                at = slice(pair * 256, pair * 256 + 256)
                score = dot_t(query, kv_v[at, h * HDIM : (h + 1) * HDIM]) * half_scale
                weight = score + score * jnp.tanh(score)
                mine = jnp.concatenate([uid == 2.0 * pair, uid == 2.0 * pair + 1.0], axis=1)
                weight = jnp.where(mine, weight, 0.0).astype(BF)
                part = dot(weight, kv_v[at, HD + h * HDIM : HD + (h + 1) * HDIM])
                total = part if total is None else total + part
            for j in range(2 * CAP):
                row_at = (j // CAP) * 12 + h * CAP + j % CAP
                ret_f[pl.ds(row_at, GSIZE, stride=MROWS), :] = total[
                    j * GSIZE : (j + 1) * GSIZE, :
                ]
        ret_msg[pl.ds(grp * GSIZE, GSIZE)] = ret_f[...].reshape(GSIZE, MROWS, HDIM).astype(BF)

    def send_back(j, carry):
        idx = (j // 32) * 32 + (j % 2) * 16 + (j % 32) // 2
        pltpu.make_async_remote_copy(
            src_ref=ret_msg.at[idx], dst_ref=ret_land.at[idx],
            send_sem=r_send.at[j // 32], recv_sem=r_recv.at[j // 32],
            device_id=peer(idx, -1), device_id_type=MESH,
        ).start()
        return carry

    first_span(land, q_recv).wait()
    attend_group(0)
    ret_land[0] = ret_msg[0]
    lax.fori_loop(1, GSIZE, send_back, 0)

    def group_step(grp, carry):
        remote_span(grp, land, q_recv).wait()
        attend_group(grp)
        lax.fori_loop(grp * GSIZE, grp * GSIZE + GSIZE, send_back, 0)
        return carry

    lax.fori_loop(1, GROUPS, group_step, 0)

    loads[4].wait()

    def own_step(i, carry):
        at = pl.ds(pl.multiple_of(i * 256, 256), 256)
        xn = xn_v[at, :]
        u_v[at, :] = silu(dot(xn, w_v[:, :HD])).astype(BF)
        own_v = silu(dot(xn, w_v[:, HD : 2 * HD])).astype(BF).astype(F32)
        own_k = silu(dot(xn, w_v[:, 3 * HD :])).astype(BF).astype(F32)
        prod = q_v[at, :].astype(F32) * own_k
        for h in range(HEADS):
            lanes = slice(h * HDIM, (h + 1) * HDIM)
            score = jnp.sum(prod[:, lanes], axis=-1, keepdims=True) * half_scale
            weight = (score + score * jnp.tanh(score)).astype(BF).astype(F32)
            att_v[at, lanes] = weight * own_v[:, lanes]
        return carry

    lax.fori_loop(0, 2, own_step, 0)
    place = (grp * 256 + (other * CAP + rank) * 32 + half * 16 + shift).astype(F32)
    place_col = jnp.sum(jnp.where(rows_i == cols_i, place, 0.0), axis=1, keepdims=True)
    lane_slot = lax.broadcasted_iota(jnp.int32, (CAND, GROUPS * 256), 1).astype(F32)
    place_v[...] = jnp.where(lane_slot == place_col, 1.0, 0.0).astype(BF)
    back_v[192:, :] = jnp.zeros((64, HD), BF)

    def hand_on(grp):
        span = pl.ds(grp * GSIZE, GSIZE)
        return pltpu.make_async_remote_copy(
            src_ref=ret_land.at[span], dst_ref=ret_sib.at[span],
            send_sem=f_send.at[grp], recv_sem=f_recv.at[grp],
            device_id=sibling, device_id_type=MESH,
        )

    def unpack(ref, grp, m):
        back_f[...] = ref[pl.ds(grp * GSIZE, GSIZE)].astype(F32).reshape(GSIZE * MROWS, HDIM)
        for s in range(CAP):
            first = (m * CAP + s) * GSIZE
            for h in range(HEADS):
                back_v[first : first + GSIZE, h * HDIM : (h + 1) * HDIM] = back_f[
                    pl.ds(c * 12 + h * CAP + s, GSIZE, stride=MROWS), :
                ].astype(BF)

    def take(grp):
        hand_on(grp).start()
        unpack(ret_land, grp, 0)
        hand_on(grp).wait()
        unpack(ret_sib, grp, 1)

    def gather(grp):
        def gather_step(i, carry):
            at = pl.ds(pl.multiple_of(i * 256, 256), 256)
            slots = pl.ds(pl.multiple_of(grp * 256, 256), 256)
            att_v[at, :] += dot(place_v[at, slots], back_v[...])
            return carry

        lax.fori_loop(0, 2, gather_step, 0)

    first_span(ret_land, r_recv).wait()
    take(0)
    gather(0)

    def take_step(grp, carry):
        remote_span(grp, ret_land, r_recv).wait()
        take(grp)
        gather(grp)
        return carry

    lax.fori_loop(1, GROUPS - 1, take_step, 0)
    remote_span(GROUPS - 1, ret_land, r_recv).wait()
    take(GROUPS - 1)

    def out_step(i, carry):
        at = pl.ds(pl.multiple_of(i * 256, 256), 256)
        last = dot(place_v[at, (GROUPS - 1) * 256 :], back_v[...])
        normed = norm_rows(att_v[at, :] + last).astype(BF).astype(F32)
        out_ref[at, :] = (normed * u_v[at, :].astype(F32)).astype(BF)
        return carry

    lax.fori_loop(0, 2, out_step, 0)

    remote_span(2, msg, q_send).wait()
    remote_span(3, msg, q_send).wait()
    first_span(ret_msg, r_send).wait()

    def sent(grp, carry):
        remote_span(grp, ret_msg, r_send).wait()
        return carry

    lax.fori_loop(1, GROUPS, sent, 0)
    pltpu.make_async_copy(ring_out.at[ring_rest], ring_out.at[ring_rest], s_send.at[0]).wait()
    pltpu.make_async_copy(plane_rest, plane_rest, s_send.at[1]).wait()


def body(history, hist_len, cand, cand_owner, cand_user, norm_gain, w_proj):
    any_spec = pl.BlockSpec(memory_space=pl.ANY)
    vmem = pl.BlockSpec(memory_space=pltpu.VMEM)
    dma = pltpu.SemaphoreType.DMA
    kv, out = pl.pallas_call(
        kernel,
        out_shape=(
            pltpu.VMEM((USERS * ROWS, 2 * HD), BF), pltpu.VMEM((CAND, HD), BF),
        ),
        in_specs=[
            pl.BlockSpec(memory_space=pltpu.SMEM), vmem, vmem, vmem, any_spec, any_spec, any_spec,
        ],
        out_specs=(vmem, vmem),
        scratch_shapes=[
            pltpu.VMEM((CAND, D), BF),
            pltpu.VMEM((USERS * ROWS, D), BF),
            pltpu.VMEM((D, 4 * HD), BF),
            pltpu.VMEM((CAND, D), BF),
            pltpu.VMEM((CAND, HD), BF),
            pltpu.VMEM((CAND, HD), BF),
            pltpu.VMEM((CAND, HD), F32),
            pltpu.VMEM((CAND, GROUPS * 256), BF),
            pltpu.VMEM((CAP, CHIPS, HD), BF),
            pltpu.VMEM((CAP, CHIPS, HD), BF),
            pltpu.VMEM((CHIPS * MROWS, HDIM), F32),
            pltpu.VMEM((CHIPS, MROWS, HDIM), BF),
            pltpu.VMEM((CHIPS, MROWS, HDIM), BF),
            pltpu.VMEM((GSIZE * MROWS, HDIM), F32),
            pltpu.VMEM((GSIZE * MROWS, HDIM), F32),
            pltpu.VMEM((CHIPS, MROWS, HDIM), BF),
            pltpu.VMEM((CHIPS, MROWS, HDIM), BF),
            pltpu.VMEM((CHIPS, MROWS, HDIM), BF),
            pltpu.VMEM((GSIZE * MROWS, HDIM), F32),
            pltpu.VMEM((256, HD), BF),
            pltpu.VMEM((8, HDIM), F32),
            pltpu.VMEM((8, HDIM), F32),
            pltpu.VMEM((8, 1, HDIM), F32),
            pltpu.VMEM((8, 1, HDIM), F32),
            pltpu.VMEM((8, HDIM), F32),
            pltpu.VMEM((HDIM, HDIM), F32),
            dma((6,)),
            dma((CAP + 1,)),
            dma((CAP + 1,)),
            pltpu.SemaphoreType.REGULAR,
            dma((GROUPS,)),
            dma((GROUPS,)),
            dma((GROUPS,)),
            dma((GROUPS,)),
            dma((GROUPS,)),
            dma((GROUPS,)),
            dma((2,)),
            dma((2,)),
        ],
        compiler_params=pltpu.CompilerParams(
            collective_id=0, has_side_effects=True, vmem_limit_bytes=58 << 20
        ),
        cost_estimate=pl.CostEstimate(
            flops=12_000_000_000, bytes_accessed=12_000_000, transcendentals=8_000_000
        ),
        name="routed_attention",
    )(
        hist_len,
        cand_owner.reshape(1, CAND),
        cand_user.reshape(1, CAND),
        norm_gain.reshape(1, D),
        cand,
        history.reshape(USERS * ROWS, D),
        w_proj,
    )
    return kv.reshape(USERS, ROWS, 2 * HD), out


def solution(mesh):
    placed = (
        P(("grp", "enc"), None, None),
        P(("grp", "enc")),
        P(("grp", "enc"), None),
        P(("grp", "enc"), None),
        P(("grp", "enc")),
        P(),
        P(),
    )
    return jax.shard_map(
        body,
        mesh=mesh,
        in_specs=placed,
        out_specs=(P(("grp", "enc"), None, None), P(("grp", "enc"), None)),
        check_vma=False,
    )
```
